32 devices in a mesh: region: 8 (over z, x), basis: 4 (over y, core).
Axes of the slice: x: 2, y: 2, z: 4, core: 2. Of those that a mesh axis runs over, the one named last changes fastest.
Arguments:
- observations: bfloat16 [262144, 128], P(('region', 'basis')), may hold values from -3 to 4
- basis_values: bfloat16 [262144, 1024], P(('region', 'basis')), as said below
- mixing: bfloat16 [1024, 1024], P('basis'), may hold values from -0.1875 to 0.1875
- pattern: int32 [8, 8], replicated, may hold values 0 or 1
- decays: float32 [8, 1024], P('region', 'basis'), may hold values from 0 to 1
- loadings: float32 [1024], P('basis'), may hold values from 0.3 to 3
Outputs:
- obs_grad: bfloat16 [262144, 128], P(('region', 'basis'))
- attenuation_slope: float32 [8, 1024], P('region', 'basis')
The draws below stay inside these ranges and needn't reach their ends.
Inputs may be any that keep to these rules, and one draw needn't show every extreme that they name: `basis_values`: every entry lies within 3.5 / 32768 ** 0.5 of zero.
All inputs are finite; a program needn't handle non-finite values.
Results may differ from the reference program's by a relative error of at most 0.015.
Values may be sent and summed in bfloat16 or wider, within the bound.
A program may use at most 128 MiB of HBM per device.

```python
import math
import jax
import jax.numpy as jnp
from jax import lax

M = 1024
BLOCK = 128
K = 128
ROWS_REG = 32768
TERRITORY_TOTAL = 8
OBS = 262144
NBLK = 8


def row_rates(key, slow_share):
    keyring = jax.random.split(jax.random.fold_in(key, 101), 3)
    slow_mask = jax.random.uniform(keyring[0], (M,)) < slow_share
    slow_rate = jnp.log(5.0) / (1.4 * TERRITORY_TOTAL) * jax.random.uniform(keyring[1], (M,), minval=0.3, maxval=1.0)
    fast_rate = jnp.exp(jax.random.uniform(keyring[2], (M,), minval=jnp.log(0.12), maxval=jnp.log(0.7)))
    return (slow_mask, jnp.where(slow_mask, slow_rate, fast_rate))


def draw_decays(key, part):
    slow_share = 0.5
    slow_mask, background_intensity = row_rates(key, slow_share)
    keyring = jax.random.split(jax.random.fold_in(key, 202), 2)
    multiplier_entries = jax.random.uniform(keyring[0], (TERRITORY_TOTAL, M), minval=0.7, maxval=1.4)
    locale_position = jax.random.randint(keyring[1], (2,), 0, TERRITORY_TOTAL)
    pulse_occurrences = jnp.sum((jnp.arange(TERRITORY_TOTAL)[:, None] == locale_position[None, :]).astype(jnp.float32), axis=1)
    summed_intensity = background_intensity[None, :] * multiplier_entries + 0.35 * pulse_occurrences[:, None]
    return jnp.exp(-summed_intensity).astype(jnp.float32)


def draw_basis_values(key, part):
    slow_share = 0.5
    slow_mask, background_intensity = row_rates(key, slow_share)
    keyring = jax.random.split(jax.random.fold_in(key, 303), 2)
    slow_weight = jax.random.uniform(keyring[0], (M,), minval=0.05, maxval=0.15)
    column_weight = jnp.where(slow_mask, slow_weight, 3.0 * (1.0 - jnp.exp(-background_intensity)))
    fluctuation = jax.random.normal(keyring[1], (OBS, M), jnp.float32)
    spread_scale = 1.0 / jnp.sqrt(jnp.float32(ROWS_REG))
    values = fluctuation * spread_scale + column_weight[None, :] / jnp.float32(ROWS_REG)
    return jnp.clip(values, -3.5 * spread_scale, 3.5 * spread_scale).astype(jnp.bfloat16)


def draw_observations(key, part):
    keyring = jax.random.split(jax.random.fold_in(key, 404), 2)
    trait_level = jax.random.uniform(keyring[0], (K,), minval=0.5, maxval=1.0)
    fluctuation = jax.random.normal(keyring[1], (OBS, K), jnp.float32)
    return jnp.clip(trait_level[None, :] + fluctuation, -3.0, 4.0).astype(jnp.bfloat16)


def place_ends(entries, rng, smallest, largest):
    dims = entries.shape
    place = [jax.random.randint(jax.random.fold_in(rng, axis), (), 0, dims[axis]) for axis in range(len(dims))]
    entries = entries.at[tuple(place)].set(smallest)
    longest = dims.index(max(dims))
    place[longest] = (place[longest] + 1) % dims[longest]
    return entries.at[tuple(place)].set(largest)


def level_of(key, extent, shards, low, top_value):
    level = 1.0
    for axis_at, parts in shards:
        draws = jax.random.uniform(jax.random.fold_in(jax.random.fold_in(key, 6), axis_at), (parts,), jnp.float32, low / len(shards), top_value / len(shards))
        level = level * jnp.repeat(jnp.exp(draws), extent[axis_at] // parts).reshape((-1,) + (1,) * (len(extent) - 1 - axis_at))
    return level


def noise(rng, dims, width, limit, shards=(), held_as=jnp.bfloat16):
    array = jax.random.normal(rng, dims, jnp.float32) * width
    if len(shards) > 0:
        array = level_of(rng, dims, shards, -0.22, 0.18) * array
    return jnp.clip(array, min=-limit, max=limit).astype(held_as)


def setup_inputs(seed: int = 0) -> dict:
    splits = jax.random.split(jax.random.key(seed), 7)
    return {
        "observations": draw_observations(jax.random.fold_in(splits[6], 71), 0),
        "basis_values": draw_basis_values(jax.random.fold_in(splits[6], 71), 0),
        "mixing": noise(splits[2], (M, M), M ** -0.5, 0.1875, ((0, 4),)),
        "pattern": place_ends((jax.random.randint(splits[3], (NBLK, NBLK), 0, 2) < 1).astype(jnp.int32), jax.random.fold_in(splits[3], 1), 0, 1),
        "decays": draw_decays(jax.random.fold_in(splits[6], 71), 0),
        "loadings": jnp.clip(jnp.exp(math.log(3.0) - 2.3025851 * jax.random.uniform(splits[5], (M,), jnp.float32) ** level_of(splits[5], (M,), ((0, 4),), -0.2, 0.2)), 0.3, 3.0),
    }


def contract_rows(first_operand, second_operand):
    return lax.dot_general(first_operand, second_operand, (((0,), (0,)), ((), ())), preferred_element_type=jnp.float32)


def block_matrix(mixing, pattern):
    blocks = jnp.arange(M) // BLOCK
    onehot = (blocks[:, None] == jnp.arange(NBLK)[None, :]).astype(jnp.float32)
    expanded = jnp.dot(jnp.dot(onehot, pattern.astype(jnp.float32)), onehot.T)
    return (jnp.eye(M, dtype=jnp.float32) + mixing.astype(jnp.float32) * expanded).astype(jnp.bfloat16)


def reference(observations, basis_values, mixing, pattern, decays, loadings):
    basis_rows = basis_values.reshape(TERRITORY_TOTAL, ROWS_REG, M)
    targets = observations.reshape(TERRITORY_TOTAL, ROWS_REG, K)
    mixer_matrix = block_matrix(mixing, pattern)

    def project_up(pairing):
        return contract_rows(pairing[0], pairing[1])

    def predict(pairing):
        return jnp.dot(pairing[0], pairing[1], preferred_element_type=jnp.float32)

    def mix_one(column):
        return jnp.dot(mixer_matrix, column, preferred_element_type=jnp.float32)

    def mix_back(column):
        return contract_rows(mixer_matrix, column)

    summary = lax.map(project_up, (basis_rows, targets)).astype(jnp.bfloat16)
    mixed_terms = lax.map(mix_one, summary)

    def upward(carried, inputs):
        factor, addend = inputs
        return factor[:, None] * carried + addend, carried

    zero_state = jnp.zeros((M, K), jnp.float32)
    _, previous = lax.scan(upward, zero_state, (decays, mixed_terms))
    states = decays[:, :, None] * previous + mixed_terms
    loaded_values = (loadings[None, :, None] * states).astype(jnp.bfloat16)
    fitted = lax.map(predict, (basis_rows, loaded_values))
    residual = (fitted - targets.astype(jnp.float32)).astype(jnp.bfloat16)
    pulled = loadings[None, :, None] * lax.map(project_up, (basis_rows, residual))

    def downward(carried, inputs):
        factor, addend = inputs
        adjoint = addend + carried
        return factor[:, None] * adjoint, adjoint

    _, adjoints = lax.scan(downward, zero_state, (decays, pulled), reverse=True)
    attenuation_slope = jnp.sum(adjoints * previous, axis=2) / K
    adjoint_b = adjoints.astype(jnp.bfloat16)
    back_mixed = lax.map(mix_back, adjoint_b).astype(jnp.bfloat16)
    spread = lax.map(predict, (basis_rows, back_mixed))
    obs_grad = (spread - residual.astype(jnp.float32)).astype(jnp.bfloat16).reshape(OBS, K)
    return obs_grad, attenuation_slope
```

```python
import functools
import math
import jax
import jax.numpy as jnp
from jax import lax
from jax.experimental import pallas as pl
from jax.experimental.pallas import tpu as pltpu
from jax.sharding import PartitionSpec as P

BLOCK = 128
CHUNKS = 8
MESH = pl.DeviceIdType.MESH


def flip(index, mask, count):
    total = 0
    for k in range(count.bit_length() - 1):
        bit = lax.rem(lax.div(index, 1 << k), 2)
        total = total + (bit if not (mask >> k) & 1 else 1 - bit) * (1 << k)
    return total


def fan_order(count):
    return sorted(range(1, count), key=lambda m: (bin(m).count("1"), -m))


def kernel(n, nr, y_hbm, phi_hbm, mix_hbm, pattern, decays, loadings, out_hbm, slope,
           phi, y, yt, mixraw, mixer, wide, rs_src, rs_dst, gathered, a_src, a_dst, s_src, s_dst,
           phi_sem, y_sem, mix_sem, out_sem, rs_send, rs_recv, ag_send, ag_recv,
           mx_send, mx_recv, a_send, a_recv, s_send, s_recv):
    b, r = lax.axis_index("basis"), lax.axis_index("region")
    steps = nr.bit_length() - 1
    _, chunks, tall, width = phi.shape
    traits = y.shape[2]
    per = width // BLOCK
    f32, bf16 = jnp.float32, jnp.bfloat16
    mate = [flip(b, m, n) for m in range(n)]
    across = [flip(r, 1 << k, nr) for k in range(steps)]
    order = list(range(n - 1, -1, -1))

    def phi_copy(m, c):
        return pltpu.make_async_copy(
            phi_hbm.at[pl.ds(pl.multiple_of(c * tall, tall), tall),
                       pl.ds(pl.multiple_of(mate[m] * width, width), width)],
            phi.at[m, c], phi_sem.at[m, c])

    def y_copy(c):
        return pltpu.make_async_copy(
            y_hbm.at[pl.ds(pl.multiple_of(c * tall, tall), tall), :], y.at[c], y_sem.at[c])

    def mix_copy(m):
        return pltpu.make_async_copy(
            mix_hbm.at[:, pl.ds(pl.multiple_of(mate[m] * width, width), width)],
            mixraw.at[m], mix_sem.at[m])

    def out_copy(c):
        return pltpu.make_async_copy(
            y.at[c], out_hbm.at[pl.ds(pl.multiple_of(c * tall, tall), tall), :], out_sem.at[c])

    for position, m in enumerate(order):
        @pl.loop(0, chunks)
        def _(c):
            if position == 0:
                y_copy(c).start()
            phi_copy(m, c).start()
        if position == 0:
            for other in range(n):
                mix_copy(other).start()

    barrier = pltpu.get_barrier_semaphore()
    for m in range(1, n):
        pl.semaphore_signal(barrier, inc=1, device_id={"basis": mate[m]}, device_id_type=MESH)
    for k in range(steps):
        pl.semaphore_signal(barrier, inc=1, device_id={"region": across[k]}, device_id_type=MESH)
    pl.semaphore_wait(barrier, n - 1 + steps)

    started = []

    def send(copy):
        copy.start()
        started.append(copy)

    def to_mate(src, dst, send_sem, recv_sem, m):
        return pltpu.make_async_remote_copy(
            src_ref=src, dst_ref=dst, send_sem=send_sem, recv_sem=recv_sem,
            device_id={"basis": mate[m]}, device_id_type=MESH)

    def to_across(src, dst, send_sem, recv_sem, k):
        return pltpu.make_async_remote_copy(
            src_ref=src, dst_ref=dst, send_sem=send_sem, recv_sem=recv_sem,
            device_id={"region": across[k]}, device_id_type=MESH)

    def gather_copy(use, m):
        low = m & -m
        return to_mate(gathered.at[use, m ^ low], gathered.at[use, m],
                       ag_send.at[use, m], ag_recv.at[use, m], low)

    def gather(use, consume):
        ready = {0}
        plan = fan_order(n)
        for m in plan:
            if bin(m).count("1") == 1:
                send(gather_copy(use, m))
        consume(0)
        for m in plan:
            source = m ^ (m & -m)
            if bin(m).count("1") > 1:
                if source not in ready:
                    gather_copy(use, source).wait_recv()
                    ready.add(source)
                send(gather_copy(use, m))
        for m in range(1, n):
            if m not in ready:
                gather_copy(use, m).wait_recv()
                ready.add(m)
            consume(m)

    def mixer_copy(m, j):
        low = m & -m
        return to_mate(mixer.at[m ^ low, j ^ low], mixer.at[m, j],
                       mx_send.at[m, j], mx_recv.at[m, j], low)

    def part_copy(use, m):
        return to_mate(rs_src.at[use, m], rs_dst.at[use, m],
                       rs_send.at[use, m], rs_recv.at[use, m], m)

    def rate_copy(k):
        return to_across(a_src.at[k], a_dst.at[k], a_send.at[k], a_recv.at[k], k)

    def scan_copy(use, k):
        return to_across(s_src.at[use, k], s_dst.at[use, k],
                         s_send.at[use, k], s_recv.at[use, k], k)

    rate = decays[...]
    load = loadings[...]
    ones = jnp.ones_like(rate)
    rates = {"own": rate, "before": ones, "after": ones}
    factors = []

    def rate_start(k):
        a_src[k] = jnp.broadcast_to(rates["own"], a_src.shape[1:])
        send(rate_copy(k))

    def rate_end(k):
        rate_copy(k).wait_recv()
        own, theirs = rates["own"], a_dst[k][0:1, :]
        before, after = rates["before"], rates["after"]
        up = jnp.full(rate.shape, lax.rem(lax.div(r, 1 << k), 2)) == 1
        factors.append((
            (jnp.where(up, 1.0, theirs), jnp.where(up, own, 1.0), jnp.where(up, before, 0.0)),
            (jnp.where(up, theirs, 1.0), jnp.where(up, 1.0, own), jnp.where(up, 0.0, after)),
        ))
        rates["before"] = jnp.where(up, theirs * before, before)
        rates["after"] = jnp.where(up, after, theirs * after)
        rates["own"] = own * theirs

    def scan(use, total):
        carried = jnp.zeros_like(total)
        for k in range(steps):
            s_src[use, k] = total.astype(bf16)
            send(scan_copy(use, k))
            keep, take, enter = factors[k][use]
            scan_copy(use, k).wait_recv()
            other = s_dst[use, k].astype(f32)
            carried = carried + enter * other
            total = keep * total + take * other
        return carried

    def build_mixer():
        rows = lax.broadcasted_iota(jnp.int32, (BLOCK, BLOCK), 0)
        columns = lax.broadcasted_iota(jnp.int32, (BLOCK, BLOCK), 1)
        eye = jnp.where(rows == columns, 1.0, 0.0).astype(f32)
        for m in range(n):
            mix_copy(m).wait()
            for i in range(per):
                for j in range(per):
                    at = (m, pl.ds(i * BLOCK, BLOCK), pl.ds(j * BLOCK, BLOCK))
                    present = pattern[b * per + i, mate[m] * per + j].astype(f32)
                    entry = mixraw[at].astype(f32) * present
                    if m == 0 and i == j:
                        entry = entry + eye
                    mixer[(0,) + at] = entry.astype(bf16)

    def turned(block):
        return block.astype(f32).T.astype(bf16)

    def project(use):
        for position, m in enumerate(order):
            def body(c, total):
                if use == 0:
                    if position == 0:
                        y_copy(c).wait()
                        yt[c] = turned(y[c])
                    phi_copy(m, c).wait()
                return total + jnp.dot(yt[c], phi[m, c], preferred_element_type=f32)

            total = lax.fori_loop(0, chunks, body, jnp.zeros((traits, width), f32))
            if m:
                rs_src[use, m] = total.astype(bf16)
                send(part_copy(use, m))
            if use == 0:
                if position == 0:
                    build_mixer()
                if position < steps:
                    rate_end(position)
                    if position + 1 < steps:
                        rate_start(position + 1)
        for m in order[:-1]:
            part_copy(use, m).wait_recv()
            total = total + rs_dst[use, m].astype(f32)
        return total

    rate_start(0)
    summary = project(0)
    for k in range(n, steps):
        rate_end(k)
        if k + 1 < steps:
            rate_start(k + 1)

    gathered[0, 0] = summary.astype(bf16)
    sums = []

    def mix_in(m):
        sums.append(lax.dot_general(gathered[0, m], mixer[0, m], (((1,), (1,)), ((), ())),
                                    preferred_element_type=f32))

    gather(0, mix_in)
    mixed = functools.reduce(jnp.add, sums)

    plan = fan_order(n)
    direct = [m for m in plan if bin(m).count("1") == 1]
    half = n // 2
    for m in direct:
        for j in range(half):
            send(mixer_copy(m, j))

    previous = scan(0, mixed)
    state = rate * previous + mixed
    gathered[1, 0] = (load * state).astype(bf16)

    def widen(m):
        wide[m] = turned(gathered[1, m])

    gather(1, widen)
    for m in direct:
        for j in range(half, n):
            send(mixer_copy(m, j))

    def predict(c):
        total = jnp.dot(phi[0, c], wide[0], preferred_element_type=f32)
        for m in range(1, n):
            total = total + jnp.dot(phi[m, c], wide[m], preferred_element_type=f32)
        return total

    @pl.loop(0, chunks)
    def _(c):
        residual = predict(c) - y[c].astype(f32)
        y[c] = residual.astype(bf16)
        yt[c] = residual.T.astype(bf16)

    seen = set()

    def mixer_there(m):
        if m and m not in seen:
            for j in range(n):
                mixer_copy(m, j).wait_recv()
            seen.add(m)

    for m in plan:
        if m not in direct:
            mixer_there(m ^ (m & -m))
            for j in range(n):
                send(mixer_copy(m, j))

    pulled = load * project(1)
    adjoint = pulled + scan(1, rate * pulled)
    gathered[2, 0] = adjoint.astype(bf16)
    slope[...] = jnp.sum(adjoint * previous, axis=0, keepdims=True) / traits
    backs = [jnp.zeros((traits, width), f32) for _ in range(n)]

    def mix_back(m):
        mixer_there(m)
        for j in range(n):
            backs[j] = backs[j] + jnp.dot(gathered[2, m], mixer[m, j], preferred_element_type=f32)

    gather(2, mix_back)
    for j in range(n):
        wide[j] = backs[j].T.astype(bf16)

    @pl.loop(0, chunks)
    def _(c):
        y[c] = (predict(c) - y[c].astype(f32)).astype(bf16)
        out_copy(c).start()

    for copy in started:
        copy.wait_send()

    @pl.loop(0, chunks)
    def _(c):
        out_copy(c).wait()


def shards(n, nr, observations, basis_values, mixing, pattern, decays, loadings):
    rows, traits = observations.shape
    width = mixing.shape[0]
    steps = nr.bit_length() - 1
    chunks, tall = CHUNKS, rows // CHUNKS
    f32, bf16 = jnp.float32, jnp.bfloat16
    dma = pltpu.SemaphoreType.DMA
    hbm = pl.BlockSpec(memory_space=pl.ANY)
    vmem = pl.BlockSpec(memory_space=pltpu.VMEM)
    return pl.pallas_call(
        functools.partial(kernel, n, nr),
        out_shape=(jax.ShapeDtypeStruct((rows, traits), bf16),
                   jax.ShapeDtypeStruct((1, width), f32)),
        in_specs=[hbm, hbm, hbm, pl.BlockSpec(memory_space=pltpu.SMEM), vmem, vmem],
        out_specs=(hbm, vmem),
        scratch_shapes=[
            pltpu.VMEM((n, chunks, tall, width), bf16),
            pltpu.VMEM((chunks, tall, traits), bf16),
            pltpu.VMEM((chunks, traits, tall), bf16),
            pltpu.VMEM((n, width, width), bf16),
            pltpu.VMEM((n, n, width, width), bf16),
            pltpu.VMEM((n, width, traits), bf16),
            pltpu.VMEM((2, n, traits, width), bf16),
            pltpu.VMEM((2, n, traits, width), bf16),
            pltpu.VMEM((3, n, traits, width), bf16),
            pltpu.VMEM((steps, 8, width), f32),
            pltpu.VMEM((steps, 8, width), f32),
            pltpu.VMEM((2, steps, traits, width), bf16),
            pltpu.VMEM((2, steps, traits, width), bf16),
            dma((n, chunks)), dma((chunks,)), dma((n,)), dma((chunks,)),
            dma((2, n)), dma((2, n)), dma((3, n)), dma((3, n)),
            dma((n, n)), dma((n, n)), dma((steps,)), dma((steps,)),
            dma((2, steps)), dma((2, steps)),
        ],
        compiler_params=pltpu.CompilerParams(
            collective_id=0, has_side_effects=True, vmem_limit_bytes=48 * 2**20),
        cost_estimate=pl.CostEstimate(
            flops=8 * rows * n * width * traits, transcendentals=0,
            bytes_accessed=2 * rows * (n * width + 2 * traits)),
    )(observations, basis_values, mixing, pattern, decays, loadings.reshape(1, width))


def solution(mesh):
    in_specs = (
        P(("region", "basis"), None),
        P(("region", "basis"), None),
        P("basis", None),
        P(),
        P("region", "basis"),
        P("basis"),
    )
    out_specs = (P(("region", "basis"), None), P("region", "basis"))
    body = functools.partial(shards, mesh.shape["basis"], mesh.shape["region"])
    return jax.shard_map(body, mesh=mesh, in_specs=in_specs, out_specs=out_specs, check_vma=False)
```

```python
import functools
import math
import jax
import jax.numpy as jnp
from jax import lax
from jax.experimental import pallas as pl
from jax.experimental.pallas import tpu as pltpu
from jax.sharding import PartitionSpec as P

BLOCK = 128
CHUNKS = 8
MESH = pl.DeviceIdType.MESH


def flip(index, mask, count):
    total = 0
    for k in range(count.bit_length() - 1):
        bit = lax.rem(lax.div(index, 1 << k), 2)
        total = total + (bit if not (mask >> k) & 1 else 1 - bit) * (1 << k)
    return total


def fan_order(count):
    return sorted(range(1, count), key=lambda m: (bin(m).count("1"), -m))


def kernel(n, nr, y_hbm, phi_hbm, mix_hbm, pattern_hbm, decays_hbm, loadings_hbm, out_hbm, slope,
           phi, y, yt, mixraw, mixer, wide, rs_src, rs_dst, gathered, a_src, a_dst, s_src, s_dst,
           pattern, decays, loadings, parts, gram_row, gram,
           phi_sem, y_sem, mix_sem, out_sem, rs_send, rs_recv, ag_send, ag_recv,
           mx_send, mx_recv, a_send, a_recv, s_send, s_recv, small_sem):
    b, r = lax.axis_index("basis"), lax.axis_index("region")
    steps = nr.bit_length() - 1
    chunks, tall, _ = phi.shape
    width = mixraw.shape[1]
    traits = y.shape[2]
    per = width // BLOCK
    f32, bf16 = jnp.float32, jnp.bfloat16
    mate = [flip(b, m, n) for m in range(n)]
    across = [flip(r, 1 << k, nr) for k in range(steps)]
    order = list(range(n - 1, -1, -1))
    half = n // 2

    def block(m, count=1):
        return pl.ds(m * width, count * width)


    def phi_copy(m, c):
        return pltpu.make_async_copy(
            phi_hbm.at[pl.ds(pl.multiple_of(c * tall, tall), tall),
                       pl.ds(pl.multiple_of(mate[m] * width, width), width)],
            phi.at[c, :, block(m)], phi_sem.at[m, c])

    def y_copy(c):
        return pltpu.make_async_copy(
            y_hbm.at[pl.ds(pl.multiple_of(c * tall, tall), tall), :], y.at[c], y_sem.at[c])

    def mix_copy(m):
        return pltpu.make_async_copy(
            mix_hbm.at[:, pl.ds(pl.multiple_of(mate[m] * width, width), width)],
            mixraw.at[m], mix_sem.at[m])

    def out_copy(c):
        return pltpu.make_async_copy(
            y.at[c], out_hbm.at[pl.ds(pl.multiple_of(c * tall, tall), tall), :], out_sem.at[c])

    small = [pltpu.make_async_copy(src, dst, small_sem.at[at]) for at, (src, dst) in enumerate(
        ((decays_hbm, decays), (loadings_hbm, loadings), (pattern_hbm, pattern)))]
    for copy in small:
        copy.start()
    for first in (half, 0):
        @pl.loop(0, chunks)
        def _(c):
            if first:
                y_copy(c).start()
            for m in range(first, first + half):
                phi_copy(m, c).start()
        if first:
            for other in range(n):
                mix_copy(other).start()

    barrier = pltpu.get_barrier_semaphore()
    for m in range(1, n):
        pl.semaphore_signal(barrier, inc=1, device_id={"basis": mate[m]}, device_id_type=MESH)
    for k in range(steps):
        pl.semaphore_signal(barrier, inc=1, device_id={"region": across[k]}, device_id_type=MESH)
    pl.semaphore_wait(barrier, n - 1 + steps)

    started = []

    def send(copy):
        copy.start()
        started.append(copy)

    def to_mate(src, dst, send_sem, recv_sem, m):
        return pltpu.make_async_remote_copy(
            src_ref=src, dst_ref=dst, send_sem=send_sem, recv_sem=recv_sem,
            device_id={"basis": mate[m]}, device_id_type=MESH)

    def to_across(src, dst, send_sem, recv_sem, k):
        return pltpu.make_async_remote_copy(
            src_ref=src, dst_ref=dst, send_sem=send_sem, recv_sem=recv_sem,
            device_id={"region": across[k]}, device_id_type=MESH)

    def gather_copy(use, m):
        low = m & -m
        return to_mate(gathered.at[use, m ^ low], gathered.at[use, m],
                       ag_send.at[use, m], ag_recv.at[use, m], low)

    def gather(use, consume, work=lambda: None):
        ready = {0}
        plan = fan_order(n)
        for m in plan:
            if bin(m).count("1") == 1:
                send(gather_copy(use, m))
        consume(0)
        for m in plan:
            source = m ^ (m & -m)
            if bin(m).count("1") > 1:
                if source not in ready:
                    work()
                    gather_copy(use, source).wait_recv()
                    ready.add(source)
                send(gather_copy(use, m))
        for m in range(1, n):
            if m not in ready:
                if m == n - 1:
                    work()
                gather_copy(use, m).wait_recv()
                ready.add(m)
            consume(m)

    def mixer_copy(m, j):
        low = m & -m
        return to_mate(mixer.at[m ^ low, j ^ low], mixer.at[m, j],
                       mx_send.at[m, j], mx_recv.at[m, j], low)

    def part_copy(use, m):
        return to_mate(rs_src.at[use, m], rs_dst.at[use, m],
                       rs_send.at[use, m], rs_recv.at[use, m], m)

    def rate_copy(k):
        return to_across(a_src.at[k], a_dst.at[k], a_send.at[k], a_recv.at[k], k)

    def scan_copy(use, k):
        return to_across(s_src.at[use, k], s_dst.at[use, k],
                         s_send.at[use, k], s_recv.at[use, k], k)

    for copy in small:
        copy.wait()
    rate = decays[...]
    load = loadings[...]
    ones = jnp.ones_like(rate)
    rates = {"own": rate, "before": ones, "after": ones}
    factors = []

    def rate_start(k):
        a_src[k] = jnp.broadcast_to(rates["own"], a_src.shape[1:])
        send(rate_copy(k))

    def rate_end(k):
        rate_copy(k).wait_recv()
        own, theirs = rates["own"], a_dst[k][0:1, :]
        before, after = rates["before"], rates["after"]
        up = jnp.full(rate.shape, lax.rem(lax.div(r, 1 << k), 2)) == 1
        factors.append((
            (jnp.where(up, 1.0, theirs), jnp.where(up, own, 1.0), jnp.where(up, before, 0.0)),
            (jnp.where(up, theirs, 1.0), jnp.where(up, 1.0, own), jnp.where(up, 0.0, after)),
        ))
        rates["before"] = jnp.where(up, theirs * before, before)
        rates["after"] = jnp.where(up, after, theirs * after)
        rates["own"] = own * theirs

    def scan(use, total, work=lambda: None):
        carried = jnp.zeros_like(total)
        for k in range(steps):
            s_src[use, k] = total.astype(bf16)
            send(scan_copy(use, k))
            keep, take, enter = factors[k][use]
            work()
            scan_copy(use, k).wait_recv()
            other = s_dst[use, k].astype(f32)
            carried = carried + enter * other
            total = keep * total + take * other
        return carried

    def build_mixer():
        rows = lax.broadcasted_iota(jnp.int32, (BLOCK, BLOCK), 0)
        columns = lax.broadcasted_iota(jnp.int32, (BLOCK, BLOCK), 1)
        eye = jnp.where(rows == columns, 1.0, 0.0).astype(f32)
        for m in range(n):
            mix_copy(m).wait()
            for i in range(per):
                for j in range(per):
                    at = (m, pl.ds(i * BLOCK, BLOCK), pl.ds(j * BLOCK, BLOCK))
                    present = pattern[b * per + i, mate[m] * per + j].astype(f32)
                    entry = mixraw[at].astype(f32) * present
                    if m == 0 and i == j:
                        entry = entry + eye
                    mixer[(0,) + at] = entry.astype(bf16)

    def turned(block):
        return block.astype(f32).T.astype(bf16)

    def send_part(use, m, value):
        rs_src[use, m] = value.astype(bf16)
        send(part_copy(use, m))

    def owned(use, total):
        for m in order[:-1]:
            part_copy(use, m).wait_recv()
            total = total + rs_dst[use, m].astype(f32)
        return total

    def project():
        for first in (half, 0):
            def body(c, total):
                if first:
                    y_copy(c).wait()
                    yt[c] = turned(y[c])
                for m in range(first, first + half):
                    phi_copy(m, c).wait()
                return total + jnp.dot(yt[c], phi[c, :, block(first, half)],
                                       preferred_element_type=f32)

            total = lax.fori_loop(0, chunks, body, jnp.zeros((traits, half * width), f32))
            for m in reversed(range(first, first + half)):
                parts[m] = total[:, (m - first) * width:(m - first + 1) * width]
                if m:
                    send_part(0, m, parts[m])
            if first:
                build_mixer()
            for k in range(0 if first else 1, 1 if first else steps):
                rate_end(k)
                if k + 1 < steps:
                    rate_start(k + 1)

    def gram_piece(m, start, stop):
        span = block(m, n - m)

        def piece():
            if start == 0:
                gram_row[:, span] = jnp.zeros((width, (n - m) * width), f32)

            @pl.loop(start, stop)
            def _(c):
                gram_row[:, span] += lax.dot_general(
                    phi[c, :, block(m)], phi[c, :, span], (((0,), (0,)), ((), ())),
                    preferred_element_type=f32)

            if stop == chunks:
                for other in range(m, n):
                    found = gram_row[:, block(other)]
                    gram[m, other] = found.astype(bf16)
                    if other != m:
                        gram[other, m] = found.T.astype(bf16)
        return piece

    cuts = {0: (0, 3, 6, chunks), 1: (0, 4, chunks)}
    pieces = []
    for m in range(n):
        cut = cuts.get(m, (0, chunks))
        pieces += [gram_piece(m, *ends) for ends in zip(cut[:-1], cut[1:])]

    def work():
        if pieces:
            pieces.pop(0)()

    rate_start(0)
    project()
    work()
    gathered[0, 0] = owned(0, parts[0]).astype(bf16)
    sums = []

    def mix_in(m):
        sums.append(lax.dot_general(gathered[0, m], mixer[0, m], (((1,), (1,)), ((), ())),
                                    preferred_element_type=f32))

    gather(0, mix_in, work)
    mixed = functools.reduce(jnp.add, sums)

    plan = fan_order(n)
    direct = [m for m in plan if bin(m).count("1") == 1]
    for m in direct:
        for j in range(half):
            send(mixer_copy(m, j))

    previous = scan(0, mixed, work)
    state = rate * previous + mixed
    gathered[1, 0] = (load * state).astype(bf16)
    gather(1, lambda m: None, work)
    while pieces:
        work()

    for m in order:
        pull = -parts[m]
        for other in range(n):
            pull = pull + jnp.dot(gathered[1, other], gram[other, m], preferred_element_type=f32)
        if m:
            send_part(1, m, pull)
    pulled = load * owned(1, pull)

    for m in direct:
        for j in range(half, n):
            send(mixer_copy(m, j))
    adjoint = pulled + scan(1, rate * pulled)
    gathered[2, 0] = adjoint.astype(bf16)
    slope[...] = jnp.sum(adjoint * previous, axis=0, keepdims=True) / traits
    backs = [-gathered[1, j].astype(f32) for j in range(n)]
    seen = set()

    def mixer_there(m):
        if m and m not in seen:
            for j in range(n):
                mixer_copy(m, j).wait_recv()
            seen.add(m)

    def mix_back(m):
        if m == 0:
            for other in plan:
                if other not in direct:
                    mixer_there(other ^ (other & -other))
                    for j in range(n):
                        send(mixer_copy(other, j))
        mixer_there(m)
        for j in range(n):
            backs[j] = backs[j] + jnp.dot(gathered[2, m], mixer[m, j], preferred_element_type=f32)

    gather(2, mix_back)
    for j in range(n):
        wide[block(j), :] = backs[j].T.astype(bf16)

    @pl.loop(0, chunks)
    def _(c):
        spread = jnp.dot(phi[c], wide[...], preferred_element_type=f32)
        y[c] = (spread + y[c].astype(f32)).astype(bf16)
        out_copy(c).start()

    for copy in started:
        copy.wait_send()

    @pl.loop(0, chunks)
    def _(c):
        out_copy(c).wait()


def shards(n, nr, observations, basis_values, mixing, pattern, decays, loadings):
    rows, traits = observations.shape
    width = mixing.shape[0]
    steps = nr.bit_length() - 1
    chunks, tall = CHUNKS, rows // CHUNKS
    f32, bf16 = jnp.float32, jnp.bfloat16
    dma = pltpu.SemaphoreType.DMA
    hbm = pl.BlockSpec(memory_space=pl.ANY)
    vmem = pl.BlockSpec(memory_space=pltpu.VMEM)
    return pl.pallas_call(
        functools.partial(kernel, n, nr),
        out_shape=(jax.ShapeDtypeStruct((rows, traits), bf16),
                   jax.ShapeDtypeStruct((1, width), f32)),
        in_specs=[hbm] * 6,
        out_specs=(hbm, vmem),
        scratch_shapes=[
            pltpu.VMEM((chunks, tall, n * width), bf16),
            pltpu.VMEM((chunks, tall, traits), bf16),
            pltpu.VMEM((chunks, traits, tall), bf16),
            pltpu.VMEM((n, width, width), bf16),
            pltpu.VMEM((n, n, width, width), bf16),
            pltpu.VMEM((n * width, traits), bf16),
            pltpu.VMEM((2, n, traits, width), bf16),
            pltpu.VMEM((2, n, traits, width), bf16),
            pltpu.VMEM((3, n, traits, width), bf16),
            pltpu.VMEM((steps, 8, width), f32),
            pltpu.VMEM((steps, 8, width), f32),
            pltpu.VMEM((2, steps, traits, width), bf16),
            pltpu.VMEM((2, steps, traits, width), bf16),
            pltpu.SMEM(pattern.shape, jnp.int32),
            pltpu.VMEM((1, width), f32),
            pltpu.VMEM((1, width), f32),
            pltpu.VMEM((n, traits, width), f32),
            pltpu.VMEM((width, n * width), f32),
            pltpu.VMEM((n, n, width, width), bf16),
            dma((n, chunks)), dma((chunks,)), dma((n,)), dma((chunks,)),
            dma((2, n)), dma((2, n)), dma((3, n)), dma((3, n)),
            dma((n, n)), dma((n, n)), dma((steps,)), dma((steps,)),
            dma((2, steps)), dma((2, steps)), dma((3,)),
        ],
        compiler_params=pltpu.CompilerParams(
            collective_id=0, has_side_effects=True, vmem_limit_bytes=60 * 2**20),
        cost_estimate=pl.CostEstimate(
            flops=8 * rows * n * width * traits, transcendentals=0,
            bytes_accessed=2 * rows * (n * width + 2 * traits)),
    )(observations, basis_values, mixing, pattern, decays, loadings.reshape(1, width))


def solution(mesh):
    in_specs = (
        P(("region", "basis"), None),
        P(("region", "basis"), None),
        P("basis", None),
        P(),
        P("region", "basis"),
        P("basis"),
    )
    out_specs = (P(("region", "basis"), None), P("region", "basis"))
    body = functools.partial(shards, mesh.shape["basis"], mesh.shape["region"])
    return jax.shard_map(body, mesh=mesh, in_specs=in_specs, out_specs=out_specs, check_vma=False)
```

```python
import functools
import math
import jax
import jax.numpy as jnp
from jax import lax
from jax.experimental import pallas as pl
from jax.experimental.pallas import tpu as pltpu
from jax.sharding import PartitionSpec as P

BLOCK = 128
CHUNKS = 8
MESH = pl.DeviceIdType.MESH


def flip(index, mask, count):
    total = 0
    for k in range(count.bit_length() - 1):
        bit = lax.rem(lax.div(index, 1 << k), 2)
        total = total + (bit if not (mask >> k) & 1 else 1 - bit) * (1 << k)
    return total


def fan_order(count):
    return sorted(range(1, count), key=lambda m: (bin(m).count("1"), -m))


def kernel(n, nr, y_hbm, phi_hbm, mix_hbm, pattern_hbm, decays_hbm, loadings_hbm, out_hbm, slope,
           phi, y, yt, mixraw, mixer, wide, rs_src, rs_dst, gathered, a_src, a_dst, s_src, s_dst,
           pattern, decays, loadings, parts, gram_row, gram,
           phi_sem, y_sem, mix_sem, out_sem, rs_send, rs_recv, ag_send, ag_recv,
           mx_send, mx_recv, a_send, a_recv, s_send, s_recv, small_sem):
    b, r = lax.axis_index("basis"), lax.axis_index("region")
    steps = nr.bit_length() - 1
    chunks, tall, _ = phi.shape
    width = mixraw.shape[1]
    traits = y.shape[2]
    per = width // BLOCK
    f32, bf16 = jnp.float32, jnp.bfloat16
    mate = [flip(b, m, n) for m in range(n)]
    across = [flip(r, 1 << k, nr) for k in range(steps)]
    order = list(range(n - 1, -1, -1))
    half = n // 2

    def block(m, count=1):
        return pl.ds(m * width, count * width)


    def phi_copy(m, c):
        return pltpu.make_async_copy(
            phi_hbm.at[pl.ds(pl.multiple_of(c * tall, tall), tall),
                       pl.ds(pl.multiple_of(mate[m] * width, width), width)],
            phi.at[c, :, block(m)], phi_sem.at[m, c])

    def y_copy(c):
        return pltpu.make_async_copy(
            y_hbm.at[pl.ds(pl.multiple_of(c * tall, tall), tall), :], y.at[c], y_sem.at[c])

    def mix_copy(m):
        return pltpu.make_async_copy(
            mix_hbm.at[:, pl.ds(pl.multiple_of(mate[m] * width, width), width)],
            mixraw.at[m], mix_sem.at[m])

    def out_copy(c):
        return pltpu.make_async_copy(
            y.at[c], out_hbm.at[pl.ds(pl.multiple_of(c * tall, tall), tall), :], out_sem.at[c])

    small = [pltpu.make_async_copy(src, dst, small_sem.at[at]) for at, (src, dst) in enumerate(
        ((decays_hbm, decays), (loadings_hbm, loadings), (pattern_hbm, pattern)))]
    for copy in small:
        copy.start()
    for first in (half, 0):
        @pl.loop(0, chunks)
        def _(c):
            if first:
                y_copy(c).start()
            for m in range(first, first + half):
                phi_copy(m, c).start()
        if first:
            for other in range(n):
                mix_copy(other).start()

    barrier = pltpu.get_barrier_semaphore()
    for m in range(1, n):
        pl.semaphore_signal(barrier, inc=1, device_id={"basis": mate[m]}, device_id_type=MESH)
    for k in range(steps):
        pl.semaphore_signal(barrier, inc=1, device_id={"region": across[k]}, device_id_type=MESH)
    pl.semaphore_wait(barrier, n - 1 + steps)

    started = []

    def send(copy):
        copy.start()
        started.append(copy)

    def to_mate(src, dst, send_sem, recv_sem, m):
        return pltpu.make_async_remote_copy(
            src_ref=src, dst_ref=dst, send_sem=send_sem, recv_sem=recv_sem,
            device_id={"basis": mate[m]}, device_id_type=MESH)

    def to_across(src, dst, send_sem, recv_sem, k):
        return pltpu.make_async_remote_copy(
            src_ref=src, dst_ref=dst, send_sem=send_sem, recv_sem=recv_sem,
            device_id={"region": across[k]}, device_id_type=MESH)

    def gather_copy(use, m):
        low = m & -m
        return to_mate(gathered.at[use, m ^ low], gathered.at[use, m],
                       ag_send.at[use, m], ag_recv.at[use, m], low)

    def gather(use, consume, work=lambda: None):
        ready = {0}
        plan = fan_order(n)
        for m in plan:
            if bin(m).count("1") == 1:
                send(gather_copy(use, m))
        consume(0)
        for m in plan:
            source = m ^ (m & -m)
            if bin(m).count("1") > 1:
                if source not in ready:
                    work()
                    gather_copy(use, source).wait_recv()
                    ready.add(source)
                send(gather_copy(use, m))
        for m in range(1, n):
            if m not in ready:
                if m == n - 1:
                    work()
                gather_copy(use, m).wait_recv()
                ready.add(m)
            consume(m)

    def mixer_copy(m, j):
        low = m & -m
        return to_mate(mixer.at[m ^ low, j ^ low], mixer.at[m, j],
                       mx_send.at[m, j], mx_recv.at[m, j], low)

    def part_copy(use, m):
        return to_mate(rs_src.at[use, m], rs_dst.at[use, m],
                       rs_send.at[use, m], rs_recv.at[use, m], m)

    def rate_copy(k):
        return to_across(a_src.at[k], a_dst.at[k], a_send.at[k], a_recv.at[k], k)

    def scan_copy(use, k):
        return to_across(s_src.at[use, k], s_dst.at[use, k],
                         s_send.at[use, k], s_recv.at[use, k], k)

    for copy in small:
        copy.wait()
    rate = decays[...]
    load = loadings[...]
    ones = jnp.ones_like(rate)
    rates = {"own": rate, "before": ones, "after": ones}
    factors = []

    def rate_start(k):
        a_src[k] = jnp.broadcast_to(rates["own"], a_src.shape[1:])
        send(rate_copy(k))

    def rate_end(k):
        rate_copy(k).wait_recv()
        own, theirs = rates["own"], a_dst[k][0:1, :]
        before, after = rates["before"], rates["after"]
        up = jnp.full(rate.shape, lax.rem(lax.div(r, 1 << k), 2)) == 1
        factors.append((
            (jnp.where(up, 1.0, theirs), jnp.where(up, own, 1.0), jnp.where(up, before, 0.0)),
            (jnp.where(up, theirs, 1.0), jnp.where(up, 1.0, own), jnp.where(up, 0.0, after)),
        ))
        rates["before"] = jnp.where(up, theirs * before, before)
        rates["after"] = jnp.where(up, after, theirs * after)
        rates["own"] = own * theirs

    def rate_step(k):
        rate_end(k)
        if k + 1 < steps:
            rate_start(k + 1)

    def scan(use, total, work=lambda: None):
        carried = jnp.zeros_like(total)
        for k in range(steps):
            s_src[use, k] = total.astype(bf16)
            send(scan_copy(use, k))
            keep, take, enter = factors[k][use]
            work()
            scan_copy(use, k).wait_recv()
            other = s_dst[use, k].astype(f32)
            carried = carried + enter * other
            total = keep * total + take * other
        return carried

    def build_mixer():
        rows = lax.broadcasted_iota(jnp.int32, (BLOCK, BLOCK), 0)
        columns = lax.broadcasted_iota(jnp.int32, (BLOCK, BLOCK), 1)
        eye = jnp.where(rows == columns, 1.0, 0.0).astype(f32)
        for m in range(n):
            mix_copy(m).wait()
            for i in range(per):
                for j in range(per):
                    at = (m, pl.ds(i * BLOCK, BLOCK), pl.ds(j * BLOCK, BLOCK))
                    present = pattern[b * per + i, mate[m] * per + j].astype(f32)
                    entry = mixraw[at].astype(f32) * present
                    if m == 0 and i == j:
                        entry = entry + eye
                    mixer[(0,) + at] = entry.astype(bf16)

    def turned(block):
        return block.astype(f32).T.astype(bf16)

    def send_part(use, m, value):
        rs_src[use, m] = value.astype(bf16)
        send(part_copy(use, m))

    def owned(use, total):
        for m in order[:-1]:
            part_copy(use, m).wait_recv()
            total = total + rs_dst[use, m].astype(f32)
        return total

    def project():
        for first in (half, 0):
            def body(c, total):
                if first:
                    y_copy(c).wait()
                    yt[c] = turned(y[c])
                for m in range(first, first + half):
                    phi_copy(m, c).wait()
                return total + jnp.dot(yt[c], phi[c, :, block(first, half)],
                                       preferred_element_type=f32)

            total = lax.fori_loop(0, chunks, body, jnp.zeros((traits, half * width), f32))
            for m in reversed(range(first, first + half)):
                parts[m] = total[:, (m - first) * width:(m - first + 1) * width]
                if m:
                    send_part(0, m, parts[m])
            if first:
                build_mixer()
                rate_step(0)

    def gram_piece(m, start, stop):
        span = block(m, n - m)

        def piece():
            if start == 0:
                gram_row[:, span] = jnp.zeros((width, (n - m) * width), f32)

            @pl.loop(start, stop)
            def _(c):
                gram_row[:, span] += lax.dot_general(
                    phi[c, :, block(m)], phi[c, :, span], (((0,), (0,)), ((), ())),
                    preferred_element_type=f32)

            if stop == chunks:
                for other in range(m, n):
                    found = gram_row[:, block(other)]
                    gram[m, other] = found.astype(bf16)
                    if other != m:
                        gram[other, m] = found.T.astype(bf16)
        return piece

    shares = [1.0, 3.0, 1.0] + [3.75] * (steps - 1) + [5.0, 2.5]
    units = [(m, c) for m in range(n) for c in range(chunks)]
    cost = sum(n - m for m, _ in units) / sum(shares)
    slots, spent, limit = [], 0.0, 0.0
    for share in shares:
        limit += share * cost
        taken = []
        while units and spent + 0.5 < limit:
            m, c = units.pop(0)
            spent += n - m
            if taken and taken[-1][0] == m:
                taken[-1][2] = c + 1
            else:
                taken.append([m, c, c + 1])
        slots.append(taken)
    slots[-1] += [[m, c, c + 1] for m, c in units]

    def work():
        if slots:
            for m, start, stop in slots.pop(0):
                gram_piece(m, start, stop)()

    rate_start(0)
    project()
    if steps > 1:
        rate_step(1)
    work()
    gathered[0, 0] = owned(0, parts[0]).astype(bf16)
    sums = []

    def mix_in(m):
        sums.append(lax.dot_general(gathered[0, m], mixer[0, m], (((1,), (1,)), ((), ())),
                                    preferred_element_type=f32))

    gather(0, mix_in, work)
    for k in range(2, steps):
        rate_step(k)
    mixed = functools.reduce(jnp.add, sums)

    plan = fan_order(n)
    direct = [m for m in plan if bin(m).count("1") == 1]
    for m in direct:
        for j in range(half):
            send(mixer_copy(m, j))

    previous = scan(0, mixed, work)
    state = rate * previous + mixed
    gathered[1, 0] = (load * state).astype(bf16)
    gather(1, lambda m: None, work)
    while slots:
        work()

    for m in order:
        pull = -parts[m]
        for other in range(n):
            pull = pull + jnp.dot(gathered[1, other], gram[other, m], preferred_element_type=f32)
        if m:
            send_part(1, m, pull)
    pulled = load * owned(1, pull)

    for m in direct:
        for j in range(half, n):
            send(mixer_copy(m, j))
    adjoint = pulled + scan(1, rate * pulled)
    gathered[2, 0] = adjoint.astype(bf16)
    slope[...] = jnp.sum(adjoint * previous, axis=0, keepdims=True) / traits
    backs = [-gathered[1, j].astype(f32) for j in range(n)]
    seen = set()

    def mixer_there(m):
        if m and m not in seen:
            for j in range(n):
                mixer_copy(m, j).wait_recv()
            seen.add(m)

    def mix_back(m):
        if m == 0:
            for other in plan:
                if other not in direct:
                    mixer_there(other ^ (other & -other))
                    for j in range(n):
                        send(mixer_copy(other, j))
        mixer_there(m)
        for j in range(n):
            backs[j] = backs[j] + jnp.dot(gathered[2, m], mixer[m, j], preferred_element_type=f32)

    gather(2, mix_back)
    for j in range(n):
        wide[block(j), :] = backs[j].T.astype(bf16)

    @pl.loop(0, chunks)
    def _(c):
        spread = jnp.dot(phi[c], wide[...], preferred_element_type=f32)
        y[c] = (spread + y[c].astype(f32)).astype(bf16)
        out_copy(c).start()

    for copy in started:
        copy.wait_send()

    @pl.loop(0, chunks)
    def _(c):
        out_copy(c).wait()


def shards(n, nr, observations, basis_values, mixing, pattern, decays, loadings):
    rows, traits = observations.shape
    width = mixing.shape[0]
    steps = nr.bit_length() - 1
    chunks, tall = CHUNKS, rows // CHUNKS
    f32, bf16 = jnp.float32, jnp.bfloat16
    dma = pltpu.SemaphoreType.DMA
    hbm = pl.BlockSpec(memory_space=pl.ANY)
    vmem = pl.BlockSpec(memory_space=pltpu.VMEM)
    return pl.pallas_call(
        functools.partial(kernel, n, nr),
        out_shape=(jax.ShapeDtypeStruct((rows, traits), bf16),
                   jax.ShapeDtypeStruct((1, width), f32)),
        in_specs=[hbm] * 6,
        out_specs=(hbm, vmem),
        scratch_shapes=[
            pltpu.VMEM((chunks, tall, n * width), bf16),
            pltpu.VMEM((chunks, tall, traits), bf16),
            pltpu.VMEM((chunks, traits, tall), bf16),
            pltpu.VMEM((n, width, width), bf16),
            pltpu.VMEM((n, n, width, width), bf16),
            pltpu.VMEM((n * width, traits), bf16),
            pltpu.VMEM((2, n, traits, width), bf16),
            pltpu.VMEM((2, n, traits, width), bf16),
            pltpu.VMEM((3, n, traits, width), bf16),
            pltpu.VMEM((steps, 8, width), f32),
            pltpu.VMEM((steps, 8, width), f32),
            pltpu.VMEM((2, steps, traits, width), bf16),
            pltpu.VMEM((2, steps, traits, width), bf16),
            pltpu.SMEM(pattern.shape, jnp.int32),
            pltpu.VMEM((1, width), f32),
            pltpu.VMEM((1, width), f32),
            pltpu.VMEM((n, traits, width), f32),
            pltpu.VMEM((width, n * width), f32),
            pltpu.VMEM((n, n, width, width), bf16),
            dma((n, chunks)), dma((chunks,)), dma((n,)), dma((chunks,)),
            dma((2, n)), dma((2, n)), dma((3, n)), dma((3, n)),
            dma((n, n)), dma((n, n)), dma((steps,)), dma((steps,)),
            dma((2, steps)), dma((2, steps)), dma((3,)),
        ],
        compiler_params=pltpu.CompilerParams(
            collective_id=0, has_side_effects=True, vmem_limit_bytes=57 * 2**20),
        cost_estimate=pl.CostEstimate(
            flops=8 * rows * n * width * traits, transcendentals=0,
            bytes_accessed=2 * rows * (n * width + 2 * traits)),
    )(observations, basis_values, mixing, pattern, decays, loadings.reshape(1, width))


def solution(mesh):
    in_specs = (
        P(("region", "basis"), None),
        P(("region", "basis"), None),
        P("basis", None),
        P(),
        P("region", "basis"),
        P("basis"),
    )
    out_specs = (P(("region", "basis"), None), P("region", "basis"))
    body = functools.partial(shards, mesh.shape["basis"], mesh.shape["region"])
    return jax.shard_map(body, mesh=mesh, in_specs=in_specs, out_specs=out_specs, check_vma=False)
```

```python
import functools
import math
import jax
import jax.numpy as jnp
from jax import lax
from jax.experimental import pallas as pl
from jax.experimental.pallas import tpu as pltpu
from jax.sharding import PartitionSpec as P

BLOCK = 128
CHUNKS = 8
SPLIT = 2
MESH = pl.DeviceIdType.MESH


def flip(index, mask, count):
    total = 0
    for k in range(count.bit_length() - 1):
        bit = lax.rem(lax.div(index, 1 << k), 2)
        total = total + (bit if not (mask >> k) & 1 else 1 - bit) * (1 << k)
    return total


def fan_order(count):
    return sorted(range(1, count), key=lambda m: (bin(m).count("1"), -m))


def kernel(n, nr, y_hbm, phi_hbm, mix_hbm, pattern_hbm, decays_hbm, loadings_hbm, out_hbm, slope,
           phi, y, yt, mixraw, mixer, wide, rs_src, rs_dst, gathered, a_src, a_dst, s_src, s_dst,
           pattern, decays, loadings, parts, gram_row, gram,
           phi_sem, y_sem, mix_sem, out_sem, rs_send, rs_recv, ag_send, ag_recv,
           mx_send, mx_recv, a_send, a_recv, s_send, s_recv, small_sem):
    b, r = lax.axis_index("basis"), lax.axis_index("region")
    steps = nr.bit_length() - 1
    chunks, tall, _ = phi.shape
    width = mixraw.shape[1]
    traits = y.shape[2]
    per = width // BLOCK
    f32, bf16 = jnp.float32, jnp.bfloat16
    mate = [flip(b, m, n) for m in range(n)]
    across = [flip(r, 1 << k, nr) for k in range(steps)]
    order = list(range(n - 1, -1, -1))
    half = n // 2
    tall_part = traits // SPLIT
    splits = range(SPLIT)

    def rows(h):
        return pl.ds(h * tall_part, tall_part)

    def block(m, count=1):
        return pl.ds(m * width, count * width)


    def phi_copy(m, c):
        return pltpu.make_async_copy(
            phi_hbm.at[pl.ds(pl.multiple_of(c * tall, tall), tall),
                       pl.ds(pl.multiple_of(mate[m] * width, width), width)],
            phi.at[c, :, block(m)], phi_sem.at[m, c])

    def y_copy(c):
        return pltpu.make_async_copy(
            y_hbm.at[pl.ds(pl.multiple_of(c * tall, tall), tall), :], y.at[c], y_sem.at[c])

    def mix_copy(m):
        return pltpu.make_async_copy(
            mix_hbm.at[:, pl.ds(pl.multiple_of(mate[m] * width, width), width)],
            mixraw.at[m], mix_sem.at[m])

    def out_copy(c):
        return pltpu.make_async_copy(
            y.at[c], out_hbm.at[pl.ds(pl.multiple_of(c * tall, tall), tall), :], out_sem.at[c])

    small = [pltpu.make_async_copy(src, dst, small_sem.at[at]) for at, (src, dst) in enumerate(
        ((decays_hbm, decays), (loadings_hbm, loadings), (pattern_hbm, pattern)))]
    for copy in small:
        copy.start()
    for first in (half, 0):
        @pl.loop(0, chunks)
        def _(c):
            if first:
                y_copy(c).start()
            for m in range(first, first + half):
                phi_copy(m, c).start()
        if first:
            for other in range(n):
                mix_copy(other).start()

    barrier = pltpu.get_barrier_semaphore()
    for m in range(1, n):
        pl.semaphore_signal(barrier, inc=1, device_id={"basis": mate[m]}, device_id_type=MESH)
    for k in range(steps):
        pl.semaphore_signal(barrier, inc=1, device_id={"region": across[k]}, device_id_type=MESH)
    pl.semaphore_wait(barrier, n - 1 + steps)

    started = []

    def send(copy):
        copy.start()
        started.append(copy)

    def to_mate(src, dst, send_sem, recv_sem, m):
        return pltpu.make_async_remote_copy(
            src_ref=src, dst_ref=dst, send_sem=send_sem, recv_sem=recv_sem,
            device_id={"basis": mate[m]}, device_id_type=MESH)

    def to_across(src, dst, send_sem, recv_sem, k):
        return pltpu.make_async_remote_copy(
            src_ref=src, dst_ref=dst, send_sem=send_sem, recv_sem=recv_sem,
            device_id={"region": across[k]}, device_id_type=MESH)

    plan = fan_order(n)
    direct = [m for m in plan if bin(m).count("1") == 1]

    def gather_copy(use, m, h):
        low = m & -m
        return to_mate(gathered.at[use, m ^ low, rows(h)], gathered.at[use, m, rows(h)],
                       ag_send.at[use, m, h], ag_recv.at[use, m, h], low)

    def gather_start(use, h, value):
        gathered[use, 0, rows(h)] = value.astype(bf16)
        for m in direct:
            send(gather_copy(use, m, h))

    def gather_finish(use, consume, work=lambda: None):
        ready = {0}
        consume(0)
        for m in plan:
            source = m ^ (m & -m)
            if m not in direct:
                if source not in ready:
                    work()
                for h in splits:
                    if source not in ready:
                        gather_copy(use, source, h).wait_recv()
                    send(gather_copy(use, m, h))
                ready.add(source)
        for m in range(1, n):
            if m not in ready:
                if m == n - 1:
                    work()
                for h in splits:
                    gather_copy(use, m, h).wait_recv()
                ready.add(m)
            consume(m)

    def mixer_copy(m, j):
        low = m & -m
        return to_mate(mixer.at[m ^ low, j ^ low], mixer.at[m, j],
                       mx_send.at[m, j], mx_recv.at[m, j], low)

    def part_copy(use, m, h):
        return to_mate(rs_src.at[use, m, rows(h)], rs_dst.at[use, m, rows(h)],
                       rs_send.at[use, m, h], rs_recv.at[use, m, h], m)

    def rate_copy(k):
        return to_across(a_src.at[k], a_dst.at[k], a_send.at[k], a_recv.at[k], k)

    def scan_copy(use, k, h):
        return to_across(s_src.at[use, k, rows(h)], s_dst.at[use, k, rows(h)],
                         s_send.at[use, k, h], s_recv.at[use, k, h], k)

    for copy in small:
        copy.wait()
    rate = decays[...]
    load = loadings[...]
    ones = jnp.ones_like(rate)
    rates = {"own": rate, "before": ones, "after": ones}
    factors = []

    def rate_start(k):
        a_src[k] = jnp.broadcast_to(rates["own"], a_src.shape[1:])
        send(rate_copy(k))

    def rate_end(k):
        rate_copy(k).wait_recv()
        own, theirs = rates["own"], a_dst[k][0:1, :]
        before, after = rates["before"], rates["after"]
        up = jnp.full(rate.shape, lax.rem(lax.div(r, 1 << k), 2)) == 1
        factors.append((
            (jnp.where(up, 1.0, theirs), jnp.where(up, own, 1.0), jnp.where(up, before, 0.0)),
            (jnp.where(up, theirs, 1.0), jnp.where(up, 1.0, own), jnp.where(up, 0.0, after)),
        ))
        rates["before"] = jnp.where(up, theirs * before, before)
        rates["after"] = jnp.where(up, after, theirs * after)
        rates["own"] = own * theirs

    def rate_step(k):
        rate_end(k)
        if k + 1 < steps:
            rate_start(k + 1)

    def scan(use, total_of, finish, work):
        totals, carried = [], []

        def leave(k, h):
            s_src[use, k, rows(h)] = totals[h].astype(bf16)
            send(scan_copy(use, k, h))

        for h in splits:
            totals.append(total_of(h))
            carried.append(jnp.zeros_like(totals[h]))
            if steps:
                leave(0, h)
        for k in range(steps):
            keep, take, enter = factors[k][use]
            work()
            for h in splits:
                scan_copy(use, k, h).wait_recv()
                other = s_dst[use, k, rows(h)].astype(f32)
                carried[h] = carried[h] + enter * other
                totals[h] = keep * totals[h] + take * other
                if k + 1 < steps:
                    leave(k + 1, h)
                else:
                    finish(h, carried[h])
        if not steps:
            for h in splits:
                finish(h, carried[h])

    def build_mixer():
        rows = lax.broadcasted_iota(jnp.int32, (BLOCK, BLOCK), 0)
        columns = lax.broadcasted_iota(jnp.int32, (BLOCK, BLOCK), 1)
        eye = jnp.where(rows == columns, 1.0, 0.0).astype(f32)
        for m in range(n):
            mix_copy(m).wait()
            for i in range(per):
                for j in range(per):
                    at = (m, pl.ds(i * BLOCK, BLOCK), pl.ds(j * BLOCK, BLOCK))
                    present = pattern[b * per + i, mate[m] * per + j].astype(f32)
                    entry = mixraw[at].astype(f32) * present
                    if m == 0 and i == j:
                        entry = entry + eye
                    mixer[(0,) + at] = entry.astype(bf16)

    def turned(block):
        return block.astype(f32).T.astype(bf16)

    def send_part(use, m, h):
        send(part_copy(use, m, h))

    def owned(use, own, h):
        total = own
        for m in order[:-1]:
            part_copy(use, m, h).wait_recv()
            total = total + rs_dst[use, m, rows(h)].astype(f32)
        return total

    def project():
        for first in (half, 0):
            def body(c, total):
                if first:
                    y_copy(c).wait()
                    yt[c] = turned(y[c])
                for m in range(first, first + half):
                    phi_copy(m, c).wait()
                return total + jnp.dot(yt[c], phi[c, :, block(first, half)],
                                       preferred_element_type=f32)

            total = lax.fori_loop(0, chunks, body, jnp.zeros((traits, half * width), f32))
            for m in reversed(range(first, first + half)):
                parts[m] = total[:, (m - first) * width:(m - first + 1) * width]
                if m:
                    rs_src[0, m] = parts[m].astype(bf16)
                    for h in splits:
                        send_part(0, m, h)
            if first:
                build_mixer()
                rate_step(0)

    def gram_piece(m, start, stop):
        span = block(m, n - m)

        def piece():
            if start == 0:
                gram_row[:, span] = jnp.zeros((width, (n - m) * width), f32)

            @pl.loop(start, stop)
            def _(c):
                gram_row[:, span] += lax.dot_general(
                    phi[c, :, block(m)], phi[c, :, span], (((0,), (0,)), ((), ())),
                    preferred_element_type=f32)

            if stop == chunks:
                for other in range(m, n):
                    found = gram_row[:, block(other)]
                    gram[m, other] = found.astype(bf16)
                    if other != m:
                        gram[other, m] = found.T.astype(bf16)
        return piece

    shares = [1.0, 3.0, 1.0] + [3.75] * (steps - 1) + [5.0, 2.5]
    units = [(m, c) for m in range(n) for c in range(chunks)]
    cost = sum(n - m for m, _ in units) / sum(shares)
    slots, spent, limit = [], 0.0, 0.0
    for share in shares:
        limit += share * cost
        taken = []
        while units and spent + 0.5 < limit:
            m, c = units.pop(0)
            spent += n - m
            if taken and taken[-1][0] == m:
                taken[-1][2] = c + 1
            else:
                taken.append([m, c, c + 1])
        slots.append(taken)
    slots[-1] += [[m, c, c + 1] for m, c in units]

    def work():
        if slots:
            for m, start, stop in slots.pop(0):
                gram_piece(m, start, stop)()

    rate_start(0)
    project()
    if steps > 1:
        rate_step(1)
    work()
    for h in splits:
        gather_start(0, h, owned(0, parts[0, rows(h)], h))
    sums = []

    def mix_in(m):
        sums.append(lax.dot_general(gathered[0, m], mixer[0, m], (((1,), (1,)), ((), ())),
                                    preferred_element_type=f32))

    gather_finish(0, mix_in, work)
    for k in range(2, steps):
        rate_step(k)
    mixed = functools.reduce(jnp.add, sums)

    def part_of(value, h):
        return value[h * tall_part:(h + 1) * tall_part]

    mixer_shares = [(m, j) for j in range(n) for m in direct]

    def spread_mixer(count):
        for _ in range(min(count, len(mixer_shares))):
            send(mixer_copy(*mixer_shares.pop(0)))

    previous = {}

    def enter(h, carried):
        previous[h] = carried
        gather_start(1, h, load * (rate * carried + part_of(mixed, h)))

    def forward_work():
        if len(mixer_shares) == n * len(direct):
            spread_mixer(half * len(direct))
        work()

    scan(0, lambda h: part_of(mixed, h), enter, forward_work)
    pulls = [-parts[m] for m in range(n)]

    def all_pulls():
        while slots:
            work()
        for m in order:
            for source in range(n):
                pulls[m] = pulls[m] + jnp.dot(gathered[1, source], gram[source, m],
                                              preferred_element_type=f32)
            if m:
                rs_src[1, m] = pulls[m].astype(bf16)
                send_part(1, m, 0)
        for h in splits[1:]:
            for m in order[:-1]:
                send_part(1, m, h)

    gather_finish(1, lambda m: None, work)
    all_pulls()
    pulled = {}

    def pulled_of(h):
        pulled[h] = load * owned(1, part_of(pulls[0], h), h)
        return rate * pulled[h]

    slopes = []

    def leave(h, carried):
        adjoint = pulled[h] + carried
        gather_start(2, h, adjoint)
        slopes.append(jnp.sum(adjoint * previous[h], axis=0, keepdims=True))

    scan(1, pulled_of, leave, lambda: spread_mixer(n * len(direct)))
    spread_mixer(n * len(direct))
    slope[...] = functools.reduce(jnp.add, slopes) / traits
    backs = [-gathered[1, j].astype(f32) for j in range(n)]
    seen = set()

    def mixer_there(m):
        if m and m not in seen:
            for j in range(n):
                mixer_copy(m, j).wait_recv()
            seen.add(m)

    def mix_back(m):
        if m == 0:
            for other in plan:
                if other not in direct:
                    mixer_there(other ^ (other & -other))
                    for j in range(n):
                        send(mixer_copy(other, j))
        mixer_there(m)
        for j in range(n):
            backs[j] = backs[j] + jnp.dot(gathered[2, m], mixer[m, j], preferred_element_type=f32)

    gather_finish(2, mix_back)
    for j in range(n):
        wide[block(j), :] = backs[j].T.astype(bf16)

    @pl.loop(0, chunks)
    def _(c):
        spread = jnp.dot(phi[c], wide[...], preferred_element_type=f32)
        y[c] = (spread + y[c].astype(f32)).astype(bf16)
        out_copy(c).start()

    for copy in started:
        copy.wait_send()

    @pl.loop(0, chunks)
    def _(c):
        out_copy(c).wait()


def shards(n, nr, observations, basis_values, mixing, pattern, decays, loadings):
    rows, traits = observations.shape
    width = mixing.shape[0]
    steps = nr.bit_length() - 1
    chunks, tall = CHUNKS, rows // CHUNKS
    f32, bf16 = jnp.float32, jnp.bfloat16
    dma = pltpu.SemaphoreType.DMA
    hbm = pl.BlockSpec(memory_space=pl.ANY)
    vmem = pl.BlockSpec(memory_space=pltpu.VMEM)
    return pl.pallas_call(
        functools.partial(kernel, n, nr),
        out_shape=(jax.ShapeDtypeStruct((rows, traits), bf16),
                   jax.ShapeDtypeStruct((1, width), f32)),
        in_specs=[hbm] * 6,
        out_specs=(hbm, vmem),
        scratch_shapes=[
            pltpu.VMEM((chunks, tall, n * width), bf16),
            pltpu.VMEM((chunks, tall, traits), bf16),
            pltpu.VMEM((chunks, traits, tall), bf16),
            pltpu.VMEM((n, width, width), bf16),
            pltpu.VMEM((n, n, width, width), bf16),
            pltpu.VMEM((n * width, traits), bf16),
            pltpu.VMEM((2, n, traits, width), bf16),
            pltpu.VMEM((2, n, traits, width), bf16),
            pltpu.VMEM((3, n, traits, width), bf16),
            pltpu.VMEM((steps, 8, width), f32),
            pltpu.VMEM((steps, 8, width), f32),
            pltpu.VMEM((2, steps, traits, width), bf16),
            pltpu.VMEM((2, steps, traits, width), bf16),
            pltpu.SMEM(pattern.shape, jnp.int32),
            pltpu.VMEM((1, width), f32),
            pltpu.VMEM((1, width), f32),
            pltpu.VMEM((n, traits, width), f32),
            pltpu.VMEM((width, n * width), f32),
            pltpu.VMEM((n, n, width, width), bf16),
            dma((n, chunks)), dma((chunks,)), dma((n,)), dma((chunks,)),
            dma((2, n, SPLIT)), dma((2, n, SPLIT)), dma((3, n, SPLIT)), dma((3, n, SPLIT)),
            dma((n, n)), dma((n, n)), dma((steps,)), dma((steps,)),
            dma((2, steps, SPLIT)), dma((2, steps, SPLIT)), dma((3,)),
        ],
        compiler_params=pltpu.CompilerParams(
            collective_id=0, has_side_effects=True, vmem_limit_bytes=57 * 2**20),
        cost_estimate=pl.CostEstimate(
            flops=8 * rows * n * width * traits, transcendentals=0,
            bytes_accessed=2 * rows * (n * width + 2 * traits)),
    )(observations, basis_values, mixing, pattern, decays, loadings.reshape(1, width))


def solution(mesh):
    in_specs = (
        P(("region", "basis"), None),
        P(("region", "basis"), None),
        P("basis", None),
        P(),
        P("region", "basis"),
        P("basis"),
    )
    out_specs = (P(("region", "basis"), None), P("region", "basis"))
    body = functools.partial(shards, mesh.shape["basis"], mesh.shape["region"])
    return jax.shard_map(body, mesh=mesh, in_specs=in_specs, out_specs=out_specs, check_vma=False)
```

```python
import functools
import math
import jax
import jax.numpy as jnp
from jax import lax
from jax.experimental import pallas as pl
from jax.experimental.pallas import tpu as pltpu
from jax.sharding import PartitionSpec as P

BLOCK = 128
CHUNKS = 8
SPLIT = 2
MESH = pl.DeviceIdType.MESH


def flip(index, mask, count):
    total = 0
    for k in range(count.bit_length() - 1):
        bit = lax.rem(lax.div(index, 1 << k), 2)
        total = total + (bit if not (mask >> k) & 1 else 1 - bit) * (1 << k)
    return total


def fan_order(count):
    return sorted(range(1, count), key=lambda m: (bin(m).count("1"), -m))


def kernel(n, nr, y_hbm, phi_hbm, mix_hbm, pattern_hbm, decays_hbm, loadings_hbm, out_hbm, slope,
           phi, y, yt, mixraw, mixer, wide, rs_src, rs_dst, gathered, a_src, a_dst, s_src, s_dst,
           pattern, decays, loadings, parts, gram_row, gram_high, gram,
           phi_sem, y_sem, mix_sem, out_sem, rs_send, rs_recv, ag_send, ag_recv,
           mx_send, mx_recv, a_send, a_recv, s_send, s_recv, small_sem):
    b, r = lax.axis_index("basis"), lax.axis_index("region")
    steps = nr.bit_length() - 1
    chunks, tall, _ = phi.shape
    width = mixraw.shape[1]
    traits = y.shape[2]
    per = width // BLOCK
    f32, bf16 = jnp.float32, jnp.bfloat16
    mate = [flip(b, m, n) for m in range(n)]
    across = [flip(r, 1 << k, nr) for k in range(steps)]
    order = list(range(n - 1, -1, -1))
    half = n // 2
    tall_part = traits // SPLIT
    splits = range(SPLIT)

    def rows(h):
        return pl.ds(h * tall_part, tall_part)

    def block(m, count=1):
        return pl.ds(m * width, count * width)


    def phi_copy(m, c):
        return pltpu.make_async_copy(
            phi_hbm.at[pl.ds(pl.multiple_of(c * tall, tall), tall),
                       pl.ds(pl.multiple_of(mate[m] * width, width), width)],
            phi.at[c, :, block(m)], phi_sem.at[m, c])

    def y_copy(c):
        return pltpu.make_async_copy(
            y_hbm.at[pl.ds(pl.multiple_of(c * tall, tall), tall), :], y.at[c], y_sem.at[c])

    def mix_copy(m):
        return pltpu.make_async_copy(
            mix_hbm.at[:, pl.ds(pl.multiple_of(mate[m] * width, width), width)],
            mixraw.at[m], mix_sem.at[m])

    def out_copy(c):
        return pltpu.make_async_copy(
            y.at[c], out_hbm.at[pl.ds(pl.multiple_of(c * tall, tall), tall), :], out_sem.at[c])

    small = [pltpu.make_async_copy(src, dst, small_sem.at[at]) for at, (src, dst) in enumerate(
        ((decays_hbm, decays), (loadings_hbm, loadings), (pattern_hbm, pattern)))]
    for copy in small:
        copy.start()
    for first in (half, 0):
        @pl.loop(0, chunks)
        def _(c):
            if first:
                y_copy(c).start()
            for m in range(first, first + half):
                phi_copy(m, c).start()
        if first:
            for other in range(n):
                mix_copy(other).start()

    barrier = pltpu.get_barrier_semaphore()
    for m in range(1, n):
        pl.semaphore_signal(barrier, inc=1, device_id={"basis": mate[m]}, device_id_type=MESH)
    for k in range(steps):
        pl.semaphore_signal(barrier, inc=1, device_id={"region": across[k]}, device_id_type=MESH)
    pl.semaphore_wait(barrier, n - 1 + steps)

    started = []

    def send(copy):
        copy.start()
        started.append(copy)

    def to_mate(src, dst, send_sem, recv_sem, m):
        return pltpu.make_async_remote_copy(
            src_ref=src, dst_ref=dst, send_sem=send_sem, recv_sem=recv_sem,
            device_id={"basis": mate[m]}, device_id_type=MESH)

    def to_across(src, dst, send_sem, recv_sem, k):
        return pltpu.make_async_remote_copy(
            src_ref=src, dst_ref=dst, send_sem=send_sem, recv_sem=recv_sem,
            device_id={"region": across[k]}, device_id_type=MESH)

    plan = fan_order(n)
    direct = [m for m in plan if bin(m).count("1") == 1]

    def gather_copy(use, m, h):
        low = m & -m
        return to_mate(gathered.at[use, m ^ low, rows(h)], gathered.at[use, m, rows(h)],
                       ag_send.at[use, m, h], ag_recv.at[use, m, h], low)

    def gather_start(use, h, value):
        gathered[use, 0, rows(h)] = value.astype(bf16)
        for m in direct:
            send(gather_copy(use, m, h))

    def gather_finish(use, consume, work=lambda: None):
        ready = {0}
        consume(0)
        for m in plan:
            source = m ^ (m & -m)
            if m not in direct:
                if source not in ready:
                    work()
                for h in splits:
                    if source not in ready:
                        gather_copy(use, source, h).wait_recv()
                    send(gather_copy(use, m, h))
                ready.add(source)
        for m in range(1, n):
            if m not in ready:
                if m == n - 1:
                    work()
                for h in splits:
                    gather_copy(use, m, h).wait_recv()
                ready.add(m)
            consume(m)

    def mixer_copy(m, j):
        low = m & -m
        return to_mate(mixer.at[m ^ low, j ^ low], mixer.at[m, j],
                       mx_send.at[m, j], mx_recv.at[m, j], low)

    def part_copy(use, m, h):
        return to_mate(rs_src.at[use, m, rows(h)], rs_dst.at[use, m, rows(h)],
                       rs_send.at[use, m, h], rs_recv.at[use, m, h], m)

    def rate_copy(k):
        return to_across(a_src.at[k], a_dst.at[k], a_send.at[k], a_recv.at[k], k)

    def scan_copy(use, k, h):
        return to_across(s_src.at[use, k, rows(h)], s_dst.at[use, k, rows(h)],
                         s_send.at[use, k, h], s_recv.at[use, k, h], k)

    for copy in small:
        copy.wait()
    rate = decays[...]
    load = loadings[...]
    ones = jnp.ones_like(rate)
    rates = {"own": rate, "before": ones, "after": ones}
    factors = []

    def rate_start(k):
        a_src[k] = jnp.broadcast_to(rates["own"], a_src.shape[1:])
        send(rate_copy(k))

    def rate_end(k):
        rate_copy(k).wait_recv()
        own, theirs = rates["own"], a_dst[k][0:1, :]
        before, after = rates["before"], rates["after"]
        up = jnp.full(rate.shape, lax.rem(lax.div(r, 1 << k), 2)) == 1
        factors.append((
            (jnp.where(up, 1.0, theirs), jnp.where(up, own, 1.0), jnp.where(up, before, 0.0)),
            (jnp.where(up, theirs, 1.0), jnp.where(up, 1.0, own), jnp.where(up, 0.0, after)),
        ))
        rates["before"] = jnp.where(up, theirs * before, before)
        rates["after"] = jnp.where(up, after, theirs * after)
        rates["own"] = own * theirs

    def rate_step(k):
        rate_end(k)
        if k + 1 < steps:
            rate_start(k + 1)

    def scan(use, total_of, finish, work):
        totals, carried = [], []

        def leave(k, h):
            s_src[use, k, rows(h)] = totals[h].astype(bf16)
            send(scan_copy(use, k, h))

        for h in splits:
            totals.append(total_of(h))
            carried.append(jnp.zeros_like(totals[h]))
            if steps:
                leave(0, h)
        for k in range(steps):
            keep, take, enter = factors[k][use]
            work()
            for h in splits:
                scan_copy(use, k, h).wait_recv()
                other = s_dst[use, k, rows(h)].astype(f32)
                carried[h] = carried[h] + enter * other
                totals[h] = keep * totals[h] + take * other
                if k + 1 < steps:
                    leave(k + 1, h)
                else:
                    finish(h, carried[h])
        if not steps:
            for h in splits:
                finish(h, carried[h])

    def build_mixer():
        rows = lax.broadcasted_iota(jnp.int32, (BLOCK, BLOCK), 0)
        columns = lax.broadcasted_iota(jnp.int32, (BLOCK, BLOCK), 1)
        eye = jnp.where(rows == columns, 1.0, 0.0).astype(f32)
        for m in range(n):
            mix_copy(m).wait()
            for i in range(per):
                for j in range(per):
                    at = (m, pl.ds(i * BLOCK, BLOCK), pl.ds(j * BLOCK, BLOCK))
                    present = pattern[b * per + i, mate[m] * per + j].astype(f32)
                    entry = mixraw[at].astype(f32) * present
                    if m == 0 and i == j:
                        entry = entry + eye
                    mixer[(0,) + at] = entry.astype(bf16)

    def turned(block):
        return block.astype(f32).T.astype(bf16)

    def send_part(use, m, h):
        send(part_copy(use, m, h))

    def owned(use, own, h):
        total = own
        for m in order[:-1]:
            part_copy(use, m, h).wait_recv()
            total = total + rs_dst[use, m, rows(h)].astype(f32)
        return total

    def cross(c, m):
        return lax.dot_general(phi[c, :, block(m)], phi[c, :, block(m, n - m)],
                               (((0,), (0,)), ((), ())), preferred_element_type=f32)

    def keep_gram(m, other, found):
        gram[m, other] = found.astype(bf16)
        if other != m:
            gram[other, m] = found.T.astype(bf16)

    def project():
        for first in (half, 0):
            if not first:
                gram_high[...] = jnp.zeros_like(gram_high)

            def body(c, total):
                if not first:
                    for m in range(half, n):
                        span = pl.ds((m - half) * width, (n - m) * width)
                        gram_high[m - half, :, span] += cross(c, m)
                if first:
                    y_copy(c).wait()
                    yt[c] = turned(y[c])
                for m in range(first, first + half):
                    phi_copy(m, c).wait()
                return total + jnp.dot(yt[c], phi[c, :, block(first, half)],
                                       preferred_element_type=f32)

            total = lax.fori_loop(0, chunks, body, jnp.zeros((traits, half * width), f32))
            for m in reversed(range(first, first + half)):
                parts[m] = total[:, (m - first) * width:(m - first + 1) * width]
                if m:
                    rs_src[0, m] = parts[m].astype(bf16)
                    for h in splits:
                        send_part(0, m, h)
            if first:
                build_mixer()
                rate_step(0)

    def gram_piece(m, start, stop):
        span = block(m, n - m)

        def piece():
            if start == 0:
                gram_row[:, span] = jnp.zeros((width, (n - m) * width), f32)

            @pl.loop(start, stop)
            def _(c):
                gram_row[:, span] += cross(c, m)

            if stop == chunks:
                for other in range(m, n):
                    keep_gram(m, other, gram_row[:, block(other)])
        return piece

    shares = [0.0, 3.0, 0.7] + [3.75] * (steps - 1) + [5.0, 2.5]
    units = [(m, c) for m in range(half) for c in range(chunks)]
    cost = sum(n - m for m, _ in units) / sum(shares)
    slots, spent, limit = [], 0.0, 0.0
    for share in shares:
        limit += share * cost
        taken = []
        while units and spent + 0.5 < limit:
            m, c = units.pop(0)
            spent += n - m
            if taken and taken[-1][0] == m:
                taken[-1][2] = c + 1
            else:
                taken.append([m, c, c + 1])
        slots.append(taken)
    slots[-1] += [[m, c, c + 1] for m, c in units]

    def work():
        if slots:
            for m, start, stop in slots.pop(0):
                gram_piece(m, start, stop)()

    rate_start(0)
    project()
    if steps > 1:
        rate_step(1)
    for m in range(half, n):
        for other in range(m, n):
            keep_gram(m, other, gram_high[m - half, :, block(other - half)])
    work()
    for h in splits:
        gather_start(0, h, owned(0, parts[0, rows(h)], h))
    sums = []

    def mix_in(m):
        sums.append(lax.dot_general(gathered[0, m], mixer[0, m], (((1,), (1,)), ((), ())),
                                    preferred_element_type=f32))

    gather_finish(0, mix_in, work)
    for k in range(2, steps):
        rate_step(k)
    mixed = functools.reduce(jnp.add, sums)

    def part_of(value, h):
        return value[h * tall_part:(h + 1) * tall_part]

    mixer_shares = [(m, j) for j in range(n) for m in direct]

    def spread_mixer(count):
        for _ in range(min(count, len(mixer_shares))):
            send(mixer_copy(*mixer_shares.pop(0)))

    previous = {}

    def enter(h, carried):
        previous[h] = carried
        gather_start(1, h, load * (rate * carried + part_of(mixed, h)))

    def forward_work():
        if len(mixer_shares) == n * len(direct):
            spread_mixer(half * len(direct))
        work()

    scan(0, lambda h: part_of(mixed, h), enter, forward_work)
    pulls = [-parts[m] for m in range(n)]

    def pull_in(source):
        for m in order:
            pulls[m] = pulls[m] + jnp.dot(gathered[1, source], gram[source, m],
                                          preferred_element_type=f32)
            if m and source == n - 1:
                rs_src[1, m] = pulls[m].astype(bf16)
                send_part(1, m, 0)

    while slots:
        work()
    gather_finish(1, pull_in)
    for h in splits[1:]:
        for m in order[:-1]:
            send_part(1, m, h)
    pulled = {}

    def pulled_of(h):
        pulled[h] = load * owned(1, part_of(pulls[0], h), h)
        return rate * pulled[h]

    slopes = []

    def leave(h, carried):
        adjoint = pulled[h] + carried
        gather_start(2, h, adjoint)
        slopes.append(jnp.sum(adjoint * previous[h], axis=0, keepdims=True))

    scan(1, pulled_of, leave, lambda: spread_mixer(n * len(direct)))
    spread_mixer(n * len(direct))
    slope[...] = functools.reduce(jnp.add, slopes) / traits
    backs = [-gathered[1, j].astype(f32) for j in range(n)]
    seen = set()

    def mixer_there(m):
        if m and m not in seen:
            for j in range(n):
                mixer_copy(m, j).wait_recv()
            seen.add(m)

    def mix_back(m):
        if m == 0:
            for other in plan:
                if other not in direct:
                    mixer_there(other ^ (other & -other))
                    for j in range(n):
                        send(mixer_copy(other, j))
        mixer_there(m)
        for j in range(n):
            backs[j] = backs[j] + jnp.dot(gathered[2, m], mixer[m, j], preferred_element_type=f32)

    gather_finish(2, mix_back)
    for j in range(n):
        wide[block(j), :] = backs[j].T.astype(bf16)

    @pl.loop(0, chunks)
    def _(c):
        spread = jnp.dot(phi[c], wide[...], preferred_element_type=f32)
        y[c] = (spread + y[c].astype(f32)).astype(bf16)
        out_copy(c).start()

    for copy in started:
        copy.wait_send()

    @pl.loop(0, chunks)
    def _(c):
        out_copy(c).wait()


def shards(n, nr, observations, basis_values, mixing, pattern, decays, loadings):
    rows, traits = observations.shape
    width = mixing.shape[0]
    steps = nr.bit_length() - 1
    chunks, tall = CHUNKS, rows // CHUNKS
    f32, bf16 = jnp.float32, jnp.bfloat16
    dma = pltpu.SemaphoreType.DMA
    hbm = pl.BlockSpec(memory_space=pl.ANY)
    vmem = pl.BlockSpec(memory_space=pltpu.VMEM)
    return pl.pallas_call(
        functools.partial(kernel, n, nr),
        out_shape=(jax.ShapeDtypeStruct((rows, traits), bf16),
                   jax.ShapeDtypeStruct((1, width), f32)),
        in_specs=[hbm] * 6,
        out_specs=(hbm, vmem),
        scratch_shapes=[
            pltpu.VMEM((chunks, tall, n * width), bf16),
            pltpu.VMEM((chunks, tall, traits), bf16),
            pltpu.VMEM((chunks, traits, tall), bf16),
            pltpu.VMEM((n, width, width), bf16),
            pltpu.VMEM((n, n, width, width), bf16),
            pltpu.VMEM((n * width, traits), bf16),
            pltpu.VMEM((2, n, traits, width), bf16),
            pltpu.VMEM((2, n, traits, width), bf16),
            pltpu.VMEM((3, n, traits, width), bf16),
            pltpu.VMEM((steps, 8, width), f32),
            pltpu.VMEM((steps, 8, width), f32),
            pltpu.VMEM((2, steps, traits, width), bf16),
            pltpu.VMEM((2, steps, traits, width), bf16),
            pltpu.SMEM(pattern.shape, jnp.int32),
            pltpu.VMEM((1, width), f32),
            pltpu.VMEM((1, width), f32),
            pltpu.VMEM((n, traits, width), f32),
            pltpu.VMEM((width, n * width), f32),
            pltpu.VMEM((n - n // 2, width, (n - n // 2) * width), f32),
            pltpu.VMEM((n, n, width, width), bf16),
            dma((n, chunks)), dma((chunks,)), dma((n,)), dma((chunks,)),
            dma((2, n, SPLIT)), dma((2, n, SPLIT)), dma((3, n, SPLIT)), dma((3, n, SPLIT)),
            dma((n, n)), dma((n, n)), dma((steps,)), dma((steps,)),
            dma((2, steps, SPLIT)), dma((2, steps, SPLIT)), dma((3,)),
        ],
        compiler_params=pltpu.CompilerParams(
            collective_id=0, has_side_effects=True, vmem_limit_bytes=57 * 2**20),
        cost_estimate=pl.CostEstimate(
            flops=8 * rows * n * width * traits, transcendentals=0,
            bytes_accessed=2 * rows * (n * width + 2 * traits)),
    )(observations, basis_values, mixing, pattern, decays, loadings.reshape(1, width))


def solution(mesh):
    in_specs = (
        P(("region", "basis"), None),
        P(("region", "basis"), None),
        P("basis", None),
        P(),
        P("region", "basis"),
        P("basis"),
    )
    out_specs = (P(("region", "basis"), None), P("region", "basis"))
    body = functools.partial(shards, mesh.shape["basis"], mesh.shape["region"])
    return jax.shard_map(body, mesh=mesh, in_specs=in_specs, out_specs=out_specs, check_vma=False)
```

```python
import functools
import math
import jax
import jax.numpy as jnp
from jax import lax
from jax.experimental import pallas as pl
from jax.experimental.pallas import tpu as pltpu
from jax.sharding import PartitionSpec as P

BLOCK = 128
CHUNKS = 8
SPLIT = 2
MESH = pl.DeviceIdType.MESH


def flip(index, mask, count):
    total = 0
    for k in range(count.bit_length() - 1):
        bit = lax.rem(lax.div(index, 1 << k), 2)
        total = total + (bit if not (mask >> k) & 1 else 1 - bit) * (1 << k)
    return total


def fan_order(count):
    return sorted(range(1, count), key=lambda m: (bin(m).count("1"), -m))


def kernel(n, nr, y_hbm, phi_hbm, mix_hbm, pattern_hbm, decays_hbm, loadings_hbm, out_hbm, slope,
           phi, y, yt, mixraw, mixer, wide, rs_src, rs_dst, gathered, a_src, a_dst, s_src, s_dst,
           pattern, decays, loadings, parts, gram_row, gram,
           phi_sem, y_sem, mix_sem, out_sem, rs_send, rs_recv, ag_send, ag_recv,
           mx_send, mx_recv, a_send, a_recv, s_send, s_recv, small_sem):
    b, r = lax.axis_index("basis"), lax.axis_index("region")
    steps = nr.bit_length() - 1
    chunks, tall, _ = phi.shape
    width = mixraw.shape[1]
    traits = y.shape[2]
    per = width // BLOCK
    f32, bf16 = jnp.float32, jnp.bfloat16
    mate = [flip(b, m, n) for m in range(n)]
    across = [flip(r, 1 << k, nr) for k in range(steps)]
    order = list(range(n - 1, -1, -1))
    half = n // 2
    tall_part = traits // SPLIT
    splits = range(SPLIT)

    def rows(h):
        return pl.ds(h * tall_part, tall_part)

    def block(m, count=1):
        return pl.ds(m * width, count * width)


    def phi_copy(m, c):
        return pltpu.make_async_copy(
            phi_hbm.at[pl.ds(pl.multiple_of(c * tall, tall), tall),
                       pl.ds(pl.multiple_of(mate[m] * width, width), width)],
            phi.at[c, :, block(m)], phi_sem.at[m, c])

    def y_copy(c):
        return pltpu.make_async_copy(
            y_hbm.at[pl.ds(pl.multiple_of(c * tall, tall), tall), :], y.at[c], y_sem.at[c])

    def mix_copy(m):
        return pltpu.make_async_copy(
            mix_hbm.at[:, pl.ds(pl.multiple_of(mate[m] * width, width), width)],
            mixraw.at[m], mix_sem.at[m])

    def out_copy(c):
        return pltpu.make_async_copy(
            y.at[c], out_hbm.at[pl.ds(pl.multiple_of(c * tall, tall), tall), :], out_sem.at[c])

    small = [pltpu.make_async_copy(src, dst, small_sem.at[at]) for at, (src, dst) in enumerate(
        ((decays_hbm, decays), (loadings_hbm, loadings), (pattern_hbm, pattern)))]
    for copy in small:
        copy.start()
    for first in (half, 0):
        @pl.loop(0, chunks)
        def _(c):
            if first:
                y_copy(c).start()
            for m in range(first, first + half):
                phi_copy(m, c).start()
        if first:
            for other in range(n):
                mix_copy(other).start()

    barrier = pltpu.get_barrier_semaphore()
    for m in range(1, n):
        pl.semaphore_signal(barrier, inc=1, device_id={"basis": mate[m]}, device_id_type=MESH)
    for k in range(steps):
        pl.semaphore_signal(barrier, inc=1, device_id={"region": across[k]}, device_id_type=MESH)
    pl.semaphore_wait(barrier, n - 1 + steps)

    started = []

    def send(copy):
        copy.start()
        started.append(copy)

    def to_mate(src, dst, send_sem, recv_sem, m):
        return pltpu.make_async_remote_copy(
            src_ref=src, dst_ref=dst, send_sem=send_sem, recv_sem=recv_sem,
            device_id={"basis": mate[m]}, device_id_type=MESH)

    def to_across(src, dst, send_sem, recv_sem, k):
        return pltpu.make_async_remote_copy(
            src_ref=src, dst_ref=dst, send_sem=send_sem, recv_sem=recv_sem,
            device_id={"region": across[k]}, device_id_type=MESH)

    plan = fan_order(n)
    direct = [m for m in plan if bin(m).count("1") == 1]

    def gather_copy(use, m, h):
        low = m & -m
        return to_mate(gathered.at[use, m ^ low, rows(h)], gathered.at[use, m, rows(h)],
                       ag_send.at[use, m, h], ag_recv.at[use, m, h], low)

    def gather_start(use, h, value):
        gathered[use, 0, rows(h)] = value.astype(bf16)
        for m in direct:
            send(gather_copy(use, m, h))

    def gather_finish(use, consume, work=lambda: None):
        ready = {0}
        consume(0)
        for m in plan:
            source = m ^ (m & -m)
            if m not in direct:
                if source not in ready:
                    work()
                for h in splits:
                    if source not in ready:
                        gather_copy(use, source, h).wait_recv()
                    send(gather_copy(use, m, h))
                ready.add(source)
        for m in range(1, n):
            if m not in ready:
                if m == n - 1:
                    work()
                for h in splits:
                    gather_copy(use, m, h).wait_recv()
                ready.add(m)
            consume(m)

    def mixer_copy(m, j):
        low = m & -m
        return to_mate(mixer.at[m ^ low, j ^ low], mixer.at[m, j],
                       mx_send.at[m, j], mx_recv.at[m, j], low)

    def part_copy(use, m, h):
        return to_mate(rs_src.at[use, m, rows(h)], rs_dst.at[use, m, rows(h)],
                       rs_send.at[use, m, h], rs_recv.at[use, m, h], m)

    def rate_copy(k):
        return to_across(a_src.at[k], a_dst.at[k], a_send.at[k], a_recv.at[k], k)

    def scan_copy(use, k, h):
        return to_across(s_src.at[use, k, rows(h)], s_dst.at[use, k, rows(h)],
                         s_send.at[use, k, h], s_recv.at[use, k, h], k)

    for copy in small:
        copy.wait()
    rate = decays[...]
    load = loadings[...]
    ones = jnp.ones_like(rate)
    rates = {"own": rate, "before": ones, "after": ones}
    factors = []

    def rate_start(k):
        a_src[k] = jnp.broadcast_to(rates["own"], a_src.shape[1:])
        send(rate_copy(k))

    def rate_end(k):
        rate_copy(k).wait_recv()
        own, theirs = rates["own"], a_dst[k][0:1, :]
        before, after = rates["before"], rates["after"]
        up = jnp.full(rate.shape, lax.rem(lax.div(r, 1 << k), 2)) == 1
        factors.append((
            (jnp.where(up, 1.0, theirs), jnp.where(up, own, 1.0), jnp.where(up, before, 0.0)),
            (jnp.where(up, theirs, 1.0), jnp.where(up, 1.0, own), jnp.where(up, 0.0, after)),
        ))
        rates["before"] = jnp.where(up, theirs * before, before)
        rates["after"] = jnp.where(up, after, theirs * after)
        rates["own"] = own * theirs

    def rate_step(k):
        rate_end(k)
        if k + 1 < steps:
            rate_start(k + 1)

    def scan(use, total_of, finish, work):
        totals, carried = [], []

        def leave(k, h):
            s_src[use, k, rows(h)] = totals[h].astype(bf16)
            send(scan_copy(use, k, h))

        for h in splits:
            totals.append(total_of(h))
            carried.append(jnp.zeros_like(totals[h]))
            if steps:
                leave(0, h)
        for k in range(steps):
            keep, take, enter = factors[k][use]
            work()
            for h in splits:
                scan_copy(use, k, h).wait_recv()
                other = s_dst[use, k, rows(h)].astype(f32)
                carried[h] = carried[h] + enter * other
                totals[h] = keep * totals[h] + take * other
                if k + 1 < steps:
                    leave(k + 1, h)
                else:
                    finish(h, carried[h])
        if not steps:
            for h in splits:
                finish(h, carried[h])

    def build_mixer():
        rows = lax.broadcasted_iota(jnp.int32, (BLOCK, BLOCK), 0)
        columns = lax.broadcasted_iota(jnp.int32, (BLOCK, BLOCK), 1)
        eye = jnp.where(rows == columns, 1.0, 0.0).astype(f32)
        for m in range(n):
            mix_copy(m).wait()
            for i in range(per):
                for j in range(per):
                    at = (m, pl.ds(i * BLOCK, BLOCK), pl.ds(j * BLOCK, BLOCK))
                    present = pattern[b * per + i, mate[m] * per + j].astype(f32)
                    entry = mixraw[at].astype(f32) * present
                    if m == 0 and i == j:
                        entry = entry + eye
                    mixer[(0,) + at] = entry.astype(bf16)

    def turned(block):
        return block.astype(f32).T.astype(bf16)

    def send_part(use, m, h):
        send(part_copy(use, m, h))

    def owned(use, own, h):
        total = own
        for m in order[:-1]:
            part_copy(use, m, h).wait_recv()
            total = total + rs_dst[use, m, rows(h)].astype(f32)
        return total

    def project():
        for first in (half, 0):
            def body(c, total):
                if first:
                    y_copy(c).wait()
                    yt[c] = turned(y[c])
                for m in range(first, first + half):
                    phi_copy(m, c).wait()
                return total + jnp.dot(yt[c], phi[c, :, block(first, half)],
                                       preferred_element_type=f32)

            total = lax.fori_loop(0, chunks, body, jnp.zeros((traits, half * width), f32))
            for m in reversed(range(first, first + half)):
                parts[m] = total[:, (m - first) * width:(m - first + 1) * width]
                if m:
                    rs_src[0, m] = parts[m].astype(bf16)
                    for h in splits:
                        send_part(0, m, h)
            if first:
                build_mixer()
                rate_step(0)

    def gram_piece(m, start, stop):
        span = block(m, n - m)

        def piece():
            if start == 0:
                gram_row[:, span] = jnp.zeros((width, (n - m) * width), f32)

            @pl.loop(start, stop)
            def _(c):
                gram_row[:, span] += lax.dot_general(
                    phi[c, :, block(m)], phi[c, :, span], (((0,), (0,)), ((), ())),
                    preferred_element_type=f32)

            if stop == chunks:
                for other in range(m, n):
                    found = gram_row[:, block(other)]
                    gram[m, other] = found.astype(bf16)
                    if other != m:
                        gram[other, m] = found.T.astype(bf16)
        return piece

    shares = [1.0, 3.0, 1.0] + [3.75] * (steps - 1) + [5.0, 2.5]
    units = [(m, c) for m in range(n) for c in range(chunks)]
    cost = sum(n - m for m, _ in units) / sum(shares)
    slots, spent, limit = [], 0.0, 0.0
    for share in shares:
        limit += share * cost
        taken = []
        while units and spent + 0.5 < limit:
            m, c = units.pop(0)
            spent += n - m
            if taken and taken[-1][0] == m:
                taken[-1][2] = c + 1
            else:
                taken.append([m, c, c + 1])
        slots.append(taken)
    slots[-1] += [[m, c, c + 1] for m, c in units]

    def work():
        if slots:
            for m, start, stop in slots.pop(0):
                gram_piece(m, start, stop)()

    rate_start(0)
    project()
    if steps > 1:
        rate_step(1)
    work()
    for h in splits:
        gather_start(0, h, owned(0, parts[0, rows(h)], h))
    sums = []

    def mix_in(m):
        sums.append(lax.dot_general(gathered[0, m], mixer[0, m], (((1,), (1,)), ((), ())),
                                    preferred_element_type=f32))

    gather_finish(0, mix_in, work)
    for k in range(2, steps):
        rate_step(k)
    mixed = functools.reduce(jnp.add, sums)

    def part_of(value, h):
        return value[h * tall_part:(h + 1) * tall_part]

    mixer_shares = [(m, j) for j in range(n) for m in direct]

    def spread_mixer(count):
        for _ in range(min(count, len(mixer_shares))):
            send(mixer_copy(*mixer_shares.pop(0)))

    previous = {}

    def enter(h, carried):
        previous[h] = carried
        gather_start(1, h, load * (rate * carried + part_of(mixed, h)))

    def forward_work():
        if len(mixer_shares) == n * len(direct):
            spread_mixer(half * len(direct))
        work()

    scan(0, lambda h: part_of(mixed, h), enter, forward_work)
    pulls = [-parts[m] for m in range(n)]

    def pull_in(source):
        for m in order:
            pulls[m] = pulls[m] + jnp.dot(gathered[1, source], gram[source, m],
                                          preferred_element_type=f32)
            if m and source == n - 1:
                rs_src[1, m] = pulls[m].astype(bf16)
                send_part(1, m, 0)

    while slots:
        work()
    gather_finish(1, pull_in)
    for h in splits[1:]:
        for m in order[:-1]:
            send_part(1, m, h)
    pulled = {}

    def pulled_of(h):
        pulled[h] = load * owned(1, part_of(pulls[0], h), h)
        return rate * pulled[h]

    slopes = []

    def leave(h, carried):
        adjoint = pulled[h] + carried
        gather_start(2, h, adjoint)
        slopes.append(jnp.sum(adjoint * previous[h], axis=0, keepdims=True))

    scan(1, pulled_of, leave, lambda: spread_mixer(n * len(direct)))
    spread_mixer(n * len(direct))
    slope[...] = functools.reduce(jnp.add, slopes) / traits
    backs = [-gathered[1, j].astype(f32) for j in range(n)]
    seen = set()

    def mixer_there(m):
        if m and m not in seen:
            for j in range(n):
                mixer_copy(m, j).wait_recv()
            seen.add(m)

    def mix_back(m):
        if m == 0:
            for other in plan:
                if other not in direct:
                    mixer_there(other ^ (other & -other))
                    for j in range(n):
                        send(mixer_copy(other, j))
        mixer_there(m)
        for j in range(n):
            backs[j] = backs[j] + jnp.dot(gathered[2, m], mixer[m, j], preferred_element_type=f32)

    gather_finish(2, mix_back)
    for j in range(n):
        wide[:, block(j)] = backs[j].astype(bf16)

    @pl.loop(0, chunks)
    def _(c):
        spread = lax.dot_general(wide[...], phi[c], (((1,), (1,)), ((), ())),
                                 preferred_element_type=f32)
        y[c] = spread.T.astype(bf16)
        out_copy(c).start()

    for copy in started:
        copy.wait_send()

    @pl.loop(0, chunks)
    def _(c):
        out_copy(c).wait()


def shards(n, nr, observations, basis_values, mixing, pattern, decays, loadings):
    rows, traits = observations.shape
    width = mixing.shape[0]
    steps = nr.bit_length() - 1
    chunks, tall = CHUNKS, rows // CHUNKS
    f32, bf16 = jnp.float32, jnp.bfloat16
    dma = pltpu.SemaphoreType.DMA
    hbm = pl.BlockSpec(memory_space=pl.ANY)
    vmem = pl.BlockSpec(memory_space=pltpu.VMEM)
    spread, slope = pl.pallas_call(
        functools.partial(kernel, n, nr),
        out_shape=(jax.ShapeDtypeStruct((rows, traits), bf16),
                   jax.ShapeDtypeStruct((1, width), f32)),
        in_specs=[hbm] * 6,
        out_specs=(hbm, vmem),
        scratch_shapes=[
            pltpu.VMEM((chunks, tall, n * width), bf16),
            pltpu.VMEM((chunks, tall, traits), bf16),
            pltpu.VMEM((chunks, traits, tall), bf16),
            pltpu.VMEM((n, width, width), bf16),
            pltpu.VMEM((n, n, width, width), bf16),
            pltpu.VMEM((traits, n * width), bf16),
            pltpu.VMEM((2, n, traits, width), bf16),
            pltpu.VMEM((2, n, traits, width), bf16),
            pltpu.VMEM((3, n, traits, width), bf16),
            pltpu.VMEM((steps, 8, width), f32),
            pltpu.VMEM((steps, 8, width), f32),
            pltpu.VMEM((2, steps, traits, width), bf16),
            pltpu.VMEM((2, steps, traits, width), bf16),
            pltpu.SMEM(pattern.shape, jnp.int32),
            pltpu.VMEM((1, width), f32),
            pltpu.VMEM((1, width), f32),
            pltpu.VMEM((n, traits, width), f32),
            pltpu.VMEM((width, n * width), f32),
            pltpu.VMEM((n, n, width, width), bf16),
            dma((n, chunks)), dma((chunks,)), dma((n,)), dma((chunks,)),
            dma((2, n, SPLIT)), dma((2, n, SPLIT)), dma((3, n, SPLIT)), dma((3, n, SPLIT)),
            dma((n, n)), dma((n, n)), dma((steps,)), dma((steps,)),
            dma((2, steps, SPLIT)), dma((2, steps, SPLIT)), dma((3,)),
        ],
        compiler_params=pltpu.CompilerParams(
            collective_id=0, has_side_effects=True, vmem_limit_bytes=57 * 2**20),
        cost_estimate=pl.CostEstimate(
            flops=8 * rows * n * width * traits, transcendentals=0,
            bytes_accessed=2 * rows * (n * width + 2 * traits)),
    )(observations, basis_values, mixing, pattern, decays, loadings.reshape(1, width))
    return (spread.astype(f32) + observations.astype(f32)).astype(bf16), slope


def solution(mesh):
    in_specs = (
        P(("region", "basis"), None),
        P(("region", "basis"), None),
        P("basis", None),
        P(),
        P("region", "basis"),
        P("basis"),
    )
    out_specs = (P(("region", "basis"), None), P("region", "basis"))
    body = functools.partial(shards, mesh.shape["basis"], mesh.shape["region"])
    return jax.shard_map(body, mesh=mesh, in_specs=in_specs, out_specs=out_specs, check_vma=False)
```

```python
import functools
import math
import jax
import jax.numpy as jnp
from jax import lax
from jax.experimental import pallas as pl
from jax.experimental.pallas import tpu as pltpu
from jax.sharding import PartitionSpec as P

BLOCK = 128
CHUNKS = 8
SPLIT = 2
TOGETHER = 2
MESH = pl.DeviceIdType.MESH


def flip(index, mask, count):
    total = 0
    for k in range(count.bit_length() - 1):
        bit = lax.rem(lax.div(index, 1 << k), 2)
        total = total + (bit if not (mask >> k) & 1 else 1 - bit) * (1 << k)
    return total


def fan_order(count):
    return sorted(range(1, count), key=lambda m: (bin(m).count("1"), -m))


def kernel(n, nr, y_hbm, phi_hbm, mix_hbm, pattern_hbm, decays_hbm, loadings_hbm, out_hbm, slope,
           phi, y, yt, mixraw, mixer, wide, rs_src, rs_dst, gathered, a_src, a_dst, s_src, s_dst,
           pattern, decays, loadings, parts, gram_row, gram,
           phi_sem, y_sem, mix_sem, out_sem, rs_send, rs_recv, ag_send, ag_recv,
           mx_send, mx_recv, a_send, a_recv, s_send, s_recv, small_sem):
    b, r = lax.axis_index("basis"), lax.axis_index("region")
    steps = nr.bit_length() - 1
    chunks, tall, _ = phi.shape
    width = mixraw.shape[1]
    traits = y.shape[2]
    per = width // BLOCK
    f32, bf16 = jnp.float32, jnp.bfloat16
    mate = [flip(b, m, n) for m in range(n)]
    across = [flip(r, 1 << k, nr) for k in range(steps)]
    order = list(range(n - 1, -1, -1))
    half = n // 2
    tall_part = traits // SPLIT
    splits = range(SPLIT)

    def rows(h):
        return pl.ds(h * tall_part, tall_part)

    def block(m, count=1):
        return pl.ds(m * width, count * width)


    def phi_copy(m, c):
        return pltpu.make_async_copy(
            phi_hbm.at[pl.ds(pl.multiple_of(c * tall, tall), tall),
                       pl.ds(pl.multiple_of(mate[m] * width, width), width)],
            phi.at[c, :, block(m)], phi_sem.at[m, c])

    def y_copy(c):
        return pltpu.make_async_copy(
            y_hbm.at[pl.ds(pl.multiple_of(c * tall, tall), tall), :], y.at[c], y_sem.at[c])

    def mix_copy(m):
        return pltpu.make_async_copy(
            mix_hbm.at[:, pl.ds(pl.multiple_of(mate[m] * width, width), width)],
            mixraw.at[m], mix_sem.at[m])

    def out_copy(c):
        return pltpu.make_async_copy(
            y.at[c], out_hbm.at[pl.ds(pl.multiple_of(c * tall, tall), tall), :], out_sem.at[c])

    small = [pltpu.make_async_copy(src, dst, small_sem.at[at]) for at, (src, dst) in enumerate(
        ((decays_hbm, decays), (loadings_hbm, loadings), (pattern_hbm, pattern)))]
    for copy in small:
        copy.start()
    for first in (half, 0):
        @pl.loop(0, chunks)
        def _(c):
            if first:
                y_copy(c).start()
            for m in range(first, first + half):
                phi_copy(m, c).start()
        if first:
            for other in range(n):
                mix_copy(other).start()

    barrier = pltpu.get_barrier_semaphore()
    for m in range(1, n):
        pl.semaphore_signal(barrier, inc=1, device_id={"basis": mate[m]}, device_id_type=MESH)
    for k in range(steps):
        pl.semaphore_signal(barrier, inc=1, device_id={"region": across[k]}, device_id_type=MESH)
    pl.semaphore_wait(barrier, n - 1 + steps)

    started = []

    def send(copy):
        copy.start()
        started.append(copy)

    def to_mate(src, dst, send_sem, recv_sem, m):
        return pltpu.make_async_remote_copy(
            src_ref=src, dst_ref=dst, send_sem=send_sem, recv_sem=recv_sem,
            device_id={"basis": mate[m]}, device_id_type=MESH)

    def to_across(src, dst, send_sem, recv_sem, k):
        return pltpu.make_async_remote_copy(
            src_ref=src, dst_ref=dst, send_sem=send_sem, recv_sem=recv_sem,
            device_id={"region": across[k]}, device_id_type=MESH)

    plan = fan_order(n)
    direct = [m for m in plan if bin(m).count("1") == 1]

    def gather_copy(use, m, h):
        low = m & -m
        return to_mate(gathered.at[use, m ^ low, rows(h)], gathered.at[use, m, rows(h)],
                       ag_send.at[use, m, h], ag_recv.at[use, m, h], low)

    def gather_start(use, h, value):
        gathered[use, 0, rows(h)] = value.astype(bf16)
        for m in direct:
            send(gather_copy(use, m, h))

    def gather_finish(use, consume, work=lambda: None):
        ready = {0}
        consume(0)
        for m in plan:
            source = m ^ (m & -m)
            if m not in direct:
                if source not in ready:
                    work()
                for h in splits:
                    if source not in ready:
                        gather_copy(use, source, h).wait_recv()
                    send(gather_copy(use, m, h))
                ready.add(source)
        for m in range(1, n):
            if m not in ready:
                if m == n - 1:
                    work()
                for h in splits:
                    gather_copy(use, m, h).wait_recv()
                ready.add(m)
            consume(m)

    def mixer_copy(m, j):
        low = m & -m
        return to_mate(mixer.at[m ^ low, j ^ low], mixer.at[m, j],
                       mx_send.at[m, j], mx_recv.at[m, j], low)

    def part_copy(use, m, h):
        return to_mate(rs_src.at[use, m, rows(h)], rs_dst.at[use, m, rows(h)],
                       rs_send.at[use, m, h], rs_recv.at[use, m, h], m)

    def rate_copy(k):
        return to_across(a_src.at[k], a_dst.at[k], a_send.at[k], a_recv.at[k], k)

    def scan_copy(use, k, h):
        return to_across(s_src.at[use, k, rows(h)], s_dst.at[use, k, rows(h)],
                         s_send.at[use, k, h], s_recv.at[use, k, h], k)

    for copy in small:
        copy.wait()
    rate = decays[...]
    load = loadings[...]
    ones = jnp.ones_like(rate)
    rates = {"own": rate, "before": ones, "after": ones}
    factors = []

    def rate_start(k):
        a_src[k] = jnp.broadcast_to(rates["own"], a_src.shape[1:])
        send(rate_copy(k))

    def rate_end(k):
        rate_copy(k).wait_recv()
        own, theirs = rates["own"], a_dst[k][0:1, :]
        before, after = rates["before"], rates["after"]
        up = jnp.full(rate.shape, lax.rem(lax.div(r, 1 << k), 2)) == 1
        factors.append((
            (jnp.where(up, 1.0, theirs), jnp.where(up, own, 1.0), jnp.where(up, before, 0.0)),
            (jnp.where(up, theirs, 1.0), jnp.where(up, 1.0, own), jnp.where(up, 0.0, after)),
        ))
        rates["before"] = jnp.where(up, theirs * before, before)
        rates["after"] = jnp.where(up, after, theirs * after)
        rates["own"] = own * theirs

    def rate_step(k):
        rate_end(k)
        if k + 1 < steps:
            rate_start(k + 1)

    def scan(use, total_of, finish, work):
        totals, carried = [], []

        def leave(k, h):
            s_src[use, k, rows(h)] = totals[h].astype(bf16)
            send(scan_copy(use, k, h))

        for h in splits:
            totals.append(total_of(h))
            carried.append(jnp.zeros_like(totals[h]))
            if steps:
                leave(0, h)
        for k in range(steps):
            keep, take, enter = factors[k][use]
            work()
            for h in splits:
                scan_copy(use, k, h).wait_recv()
                other = s_dst[use, k, rows(h)].astype(f32)
                carried[h] = carried[h] + enter * other
                totals[h] = keep * totals[h] + take * other
                if k + 1 < steps:
                    leave(k + 1, h)
                else:
                    finish(h, carried[h])
        if not steps:
            for h in splits:
                finish(h, carried[h])

    def build_mixer():
        rows = lax.broadcasted_iota(jnp.int32, (BLOCK, BLOCK), 0)
        columns = lax.broadcasted_iota(jnp.int32, (BLOCK, BLOCK), 1)
        eye = jnp.where(rows == columns, 1.0, 0.0).astype(f32)
        for m in range(n):
            mix_copy(m).wait()
            for i in range(per):
                for j in range(per):
                    at = (m, pl.ds(i * BLOCK, BLOCK), pl.ds(j * BLOCK, BLOCK))
                    present = pattern[b * per + i, mate[m] * per + j].astype(f32)
                    entry = mixraw[at].astype(f32) * present
                    if m == 0 and i == j:
                        entry = entry + eye
                    mixer[(0,) + at] = entry.astype(bf16)

    def turned(block):
        return block.astype(f32).T.astype(bf16)

    def send_part(use, m, h):
        send(part_copy(use, m, h))

    def owned(use, own, h):
        total = own
        for m in order[:-1]:
            part_copy(use, m, h).wait_recv()
            total = total + rs_dst[use, m, rows(h)].astype(f32)
        return total

    def project():
        for first in (half, 0):
            def body(c, total):
                if first:
                    y_copy(c).wait()
                    yt[c] = turned(y[c])
                for m in range(first, first + half):
                    phi_copy(m, c).wait()
                return total + jnp.dot(yt[c], phi[c, :, block(first, half)],
                                       preferred_element_type=f32)

            total = lax.fori_loop(0, chunks, body, jnp.zeros((traits, half * width), f32))
            for m in reversed(range(first, first + half)):
                parts[m] = total[:, (m - first) * width:(m - first + 1) * width]
                if m:
                    rs_src[0, m] = parts[m].astype(bf16)
                    for h in splits:
                        send_part(0, m, h)
            if first:
                build_mixer()
                rate_step(0)

    def gram_piece(m, start, stop):
        span = block(m, n - m)

        def piece():
            if start == 0:
                gram_row[:, span] = jnp.zeros((width, (n - m) * width), f32)

            @pl.loop(start, stop)
            def _(c):
                gram_row[:, span] += lax.dot_general(
                    phi[c, :, block(m)], phi[c, :, span], (((0,), (0,)), ((), ())),
                    preferred_element_type=f32)

            if stop == chunks:
                for other in range(m, n):
                    found = gram_row[:, block(other)]
                    gram[m, other] = found.astype(bf16)
                    if other != m:
                        gram[other, m] = found.T.astype(bf16)
        return piece

    shares = [1.0, 3.0, 1.0] + [3.75] * (steps - 1) + [5.0, 2.5]
    units = [(m, c) for m in range(n) for c in range(chunks)]
    cost = sum(n - m for m, _ in units) / sum(shares)
    slots, spent, limit = [], 0.0, 0.0
    for share in shares:
        limit += share * cost
        taken = []
        while units and spent + 0.5 < limit:
            m, c = units.pop(0)
            spent += n - m
            if taken and taken[-1][0] == m:
                taken[-1][2] = c + 1
            else:
                taken.append([m, c, c + 1])
        slots.append(taken)
    slots[-1] += [[m, c, c + 1] for m, c in units]

    def work():
        if slots:
            for m, start, stop in slots.pop(0):
                gram_piece(m, start, stop)()

    rate_start(0)
    project()
    if steps > 1:
        rate_step(1)
    work()
    for h in splits:
        gather_start(0, h, owned(0, parts[0, rows(h)], h))
    sums = []

    def mix_in(m):
        sums.append(lax.dot_general(gathered[0, m], mixer[0, m], (((1,), (1,)), ((), ())),
                                    preferred_element_type=f32))

    gather_finish(0, mix_in, work)
    for k in range(2, steps):
        rate_step(k)
    mixed = functools.reduce(jnp.add, sums)

    def part_of(value, h):
        return value[h * tall_part:(h + 1) * tall_part]

    mixer_shares = [(m, j) for j in range(n) for m in direct]

    def spread_mixer(count):
        for _ in range(min(count, len(mixer_shares))):
            send(mixer_copy(*mixer_shares.pop(0)))

    previous = {}

    def enter(h, carried):
        previous[h] = carried
        gather_start(1, h, load * (rate * carried + part_of(mixed, h)))

    def forward_work():
        if len(mixer_shares) == n * len(direct):
            spread_mixer(half * len(direct))
        work()

    scan(0, lambda h: part_of(mixed, h), enter, forward_work)
    pulls = [-parts[m] for m in range(n)]

    def pull_in(source):
        for m in order:
            pulls[m] = pulls[m] + jnp.dot(gathered[1, source], gram[source, m],
                                          preferred_element_type=f32)
            if m and source == n - 1:
                rs_src[1, m] = pulls[m].astype(bf16)
                send_part(1, m, 0)

    while slots:
        work()
    gather_finish(1, pull_in)
    for h in splits[1:]:
        for m in order[:-1]:
            send_part(1, m, h)
    pulled = {}

    def pulled_of(h):
        pulled[h] = load * owned(1, part_of(pulls[0], h), h)
        return rate * pulled[h]

    slopes = []

    def leave(h, carried):
        adjoint = pulled[h] + carried
        gather_start(2, h, adjoint)
        slopes.append(jnp.sum(adjoint * previous[h], axis=0, keepdims=True))

    scan(1, pulled_of, leave, lambda: spread_mixer(n * len(direct)))
    spread_mixer(n * len(direct))
    slope[...] = functools.reduce(jnp.add, slopes) / traits
    backs = [-gathered[1, j].astype(f32) for j in range(n)]
    seen = set()

    def mixer_there(m):
        if m and m not in seen:
            for j in range(n):
                mixer_copy(m, j).wait_recv()
            seen.add(m)

    def mix_back(m):
        if m == 0:
            for other in plan:
                if other not in direct:
                    mixer_there(other ^ (other & -other))
                    for j in range(n):
                        send(mixer_copy(other, j))
        mixer_there(m)
        for j in range(n):
            backs[j] = backs[j] + jnp.dot(gathered[2, m], mixer[m, j], preferred_element_type=f32)

    gather_finish(2, mix_back)
    for j in range(n):
        wide[block(j), :] = backs[j].T.astype(bf16)

    @pl.loop(0, chunks // TOGETHER)
    def _(turn):
        for at in range(TOGETHER):
            c = turn * TOGETHER + at
            spread = jnp.dot(phi[c], wide[...], preferred_element_type=f32)
            y[c] = (spread + y[c].astype(f32)).astype(bf16)
        for at in range(TOGETHER):
            out_copy(turn * TOGETHER + at).start()

    for copy in started:
        copy.wait_send()

    @pl.loop(0, chunks)
    def _(c):
        out_copy(c).wait()


def shards(n, nr, observations, basis_values, mixing, pattern, decays, loadings):
    rows, traits = observations.shape
    width = mixing.shape[0]
    steps = nr.bit_length() - 1
    chunks, tall = CHUNKS, rows // CHUNKS
    f32, bf16 = jnp.float32, jnp.bfloat16
    dma = pltpu.SemaphoreType.DMA
    hbm = pl.BlockSpec(memory_space=pl.ANY)
    vmem = pl.BlockSpec(memory_space=pltpu.VMEM)
    return pl.pallas_call(
        functools.partial(kernel, n, nr),
        out_shape=(jax.ShapeDtypeStruct((rows, traits), bf16),
                   jax.ShapeDtypeStruct((1, width), f32)),
        in_specs=[hbm] * 6,
        out_specs=(hbm, vmem),
        scratch_shapes=[
            pltpu.VMEM((chunks, tall, n * width), bf16),
            pltpu.VMEM((chunks, tall, traits), bf16),
            pltpu.VMEM((chunks, traits, tall), bf16),
            pltpu.VMEM((n, width, width), bf16),
            pltpu.VMEM((n, n, width, width), bf16),
            pltpu.VMEM((n * width, traits), bf16),
            pltpu.VMEM((2, n, traits, width), bf16),
            pltpu.VMEM((2, n, traits, width), bf16),
            pltpu.VMEM((3, n, traits, width), bf16),
            pltpu.VMEM((steps, 8, width), f32),
            pltpu.VMEM((steps, 8, width), f32),
            pltpu.VMEM((2, steps, traits, width), bf16),
            pltpu.VMEM((2, steps, traits, width), bf16),
            pltpu.SMEM(pattern.shape, jnp.int32),
            pltpu.VMEM((1, width), f32),
            pltpu.VMEM((1, width), f32),
            pltpu.VMEM((n, traits, width), f32),
            pltpu.VMEM((width, n * width), f32),
            pltpu.VMEM((n, n, width, width), bf16),
            dma((n, chunks)), dma((chunks,)), dma((n,)), dma((chunks,)),
            dma((2, n, SPLIT)), dma((2, n, SPLIT)), dma((3, n, SPLIT)), dma((3, n, SPLIT)),
            dma((n, n)), dma((n, n)), dma((steps,)), dma((steps,)),
            dma((2, steps, SPLIT)), dma((2, steps, SPLIT)), dma((3,)),
        ],
        compiler_params=pltpu.CompilerParams(
            collective_id=0, has_side_effects=True, vmem_limit_bytes=57 * 2**20),
        cost_estimate=pl.CostEstimate(
            flops=8 * rows * n * width * traits, transcendentals=0,
            bytes_accessed=2 * rows * (n * width + 2 * traits)),
    )(observations, basis_values, mixing, pattern, decays, loadings.reshape(1, width))


def solution(mesh):
    in_specs = (
        P(("region", "basis"), None),
        P(("region", "basis"), None),
        P("basis", None),
        P(),
        P("region", "basis"),
        P("basis"),
    )
    out_specs = (P(("region", "basis"), None), P("region", "basis"))
    body = functools.partial(shards, mesh.shape["basis"], mesh.shape["region"])
    return jax.shard_map(body, mesh=mesh, in_specs=in_specs, out_specs=out_specs, check_vma=False)
```
